128 devices in a mesh: row: 16 (over z, x_hi, core), col: 8 (over y, x_lo).
Axes of the slice: x: 4 (x_hi: 2, x_lo: 2; x = x_hi * 2 + x_lo), y: 4, z: 4, core: 2. Of those that a mesh axis runs over, the one named last changes fastest.
Arguments:
- pair_state: float32 [768, 768, 128], P('row', 'col'), may hold values from -120 to 120
- pair_mask: int32 [768, 768], P('row', 'col'), may hold values 0 or 1
- chain_ids: int32 [768], replicated, may hold values from 0 to 5, never falling along the last dimension, each value on 1 to 256 neighbouring positions
- ln_gain: float32 [2, 128], replicated, may hold values from 0.25 to 1.75
- w_proj: float32 [2, 128, 512], replicated, may hold values from -0.5 to 0.5
- w_bias: float32 [2, 128, 4], replicated, may hold values from -35.35534 to 35.35534
- w_out: float32 [2, 128, 128], replicated, may hold values from -1.8 to 1.8
- chain_gain: float32 [2, 4], replicated, may hold values from -4 to 4
Outputs:
- pair_out: float32 [768, 768, 128], P('row', 'col')
The draws below stay inside these ranges and needn't reach their ends.
All inputs are finite; a program needn't handle non-finite values. No bound on the sum of `pair_mask` on one device may be relied on, other than what follows from the above.
Results may differ from the reference program's by a relative error of at most 0.0003.
Values sent between devices are 32-bit elements; how exact they have to be, the bound alone decides.
No kernel may reach another device: no remote copies, remote signals or barrier semaphores. Data moves between devices by JAX's collectives and lax.ppermute only.
A program may use at most 128 MiB of HBM per device.

```python
import math
import jax
import jax.numpy as jnp
import numpy as np
from jax import lax

C = 128
H = 4
RES = 768


def draw_pair_state(key, part):
    key = jax.random.fold_in(key, 11)
    key_base, key_chan = jax.random.split(key, 2)
    noise_base = jax.random.truncated_normal(key_base, -4.0, 4.0, (RES, RES, C), jnp.float32)
    channel = jnp.exp(jax.random.uniform(key_chan, (C,), jnp.float32, 0.0, math.log(4.0)))
    return noise_base * channel


def draw_w_bias(key, part):
    key = jax.random.fold_in(key, 12)
    spread = 1.5
    return jax.random.truncated_normal(key, -4.0, 4.0, (2, C, H), jnp.float32) * spread / math.sqrt(C)


def set_ends(values, key, smallest, high):
    place = [jax.random.randint(jax.random.fold_in(key, axis), (), 0, length) for axis, length in enumerate(values.shape)]
    main_axis = values.shape.index(max(values.shape))
    beside = place[:main_axis] + [(place[main_axis] + 1) % values.shape[main_axis]] + place[main_axis + 1:]
    return values.at[tuple(place)].set(smallest).at[tuple(beside)].set(high)


def length_profile(number_of, total, limit, lean):
    portions = [(1 << 20) // math.isqrt(grade ** lean) + 1 for grade in range(2, number_of + 1)]
    spare, holding = total - limit - (number_of - 1), [1] * (number_of - 1)
    while spare > 0:
        movable = [i for i in range(number_of - 1) if holding[i] < limit]
        pool, remaining = sum([portions[i] for i in movable]), spare
        for i in movable:
            more = min(limit - holding[i], max(1, remaining * portions[i] // pool), spare)
            holding[i] = holding[i] + more
            spare = spare - more
    return np.array([limit] + holding)


def ragged_sizes(key, count, total, bound, skew):
    if count == 2:
        one = jax.random.randint(key, (), max(1, total - bound), min(bound, total - 1) + 1)
        return jnp.stack([one, total - one])
    sizes = jnp.asarray(length_profile(count, total, bound, skew), jnp.int32)
    twos = (count - 1) // 2
    source_of, receiver = sizes[1:1 + 2 * twos:2], sizes[2:2 + 2 * twos:2]
    room = jnp.minimum(source_of - 1, bound - receiver)
    shifted = jax.random.randint(jax.random.fold_in(key, 1), (twos,), 0, 1 << 20) % (room + 1)
    sizes = sizes.at[1:1 + 2 * twos:2].set(source_of - shifted).at[2:2 + 2 * twos:2].set(receiver + shifted)
    return sizes[jax.random.permutation(jax.random.fold_in(key, 2), count)]


def bell_draw(rng, extent, scale, bound, kind=jnp.bfloat16):
    result = jax.random.normal(rng, extent, jnp.float32) * scale
    return jnp.minimum(jnp.maximum(result, -bound), bound).astype(kind)


def setup_inputs(seed: int = 0) -> dict:
    streams_of = jax.random.split(jax.random.key(seed), 9)
    pair_state = draw_pair_state(jax.random.fold_in(streams_of[8], 71), 0)
    pair_mask = set_ends((jax.random.randint(streams_of[1], (RES, RES), 0, 8) < 7).astype(jnp.int32), jax.random.fold_in(streams_of[1], 1), 0, 1)
    chain_ids = jnp.searchsorted(jnp.cumsum(ragged_sizes(streams_of[2], 6, RES, RES // 3, 1)), jnp.arange(RES), side="right").astype(jnp.int32)
    ln_gain = jnp.clip(1.0 + 0.15 * jax.random.normal(streams_of[3], (2, C), jnp.float32), 0.25, 1.75)
    w_proj = bell_draw(streams_of[4], (2, C, 4 * C), C ** -0.5, 0.5, jnp.float32)
    w_bias = draw_w_bias(jax.random.fold_in(streams_of[8], 71), 0)
    w_out = bell_draw(streams_of[6], (2, C, C), 0.3, 1.8, jnp.float32)
    chain_gain = bell_draw(streams_of[7], (2, H), 1.0, 4.0, jnp.float32)
    return dict(pair_state=pair_state, pair_mask=pair_mask, chain_ids=chain_ids, ln_gain=ln_gain, w_proj=w_proj, w_bias=w_bias, w_out=w_out, chain_gain=chain_gain)


def layer_norm(values, scales):
    average = lax.optimization_barrier(jnp.mean(values, axis=-1, keepdims=True))
    centred = values - average
    variance = lax.optimization_barrier(jnp.mean(centred * centred, axis=-1, keepdims=True))
    return centred * lax.rsqrt(variance + 1e-05) * scales

def attend_row(normed_row, mask_row, bias_plane, w_proj, w_out):
    width = normed_row.shape[1]
    head_count = bias_plane.shape[0]
    head_size = width // head_count
    projected = jnp.dot(normed_row, w_proj, precision=lax.Precision.HIGHEST)
    query_proj = projected[:, :width].reshape(-1, head_count, head_size) * head_size ** (-0.5)
    key_proj = projected[:, width:2 * width].reshape(-1, head_count, head_size)
    value_proj = projected[:, 2 * width:3 * width].reshape(-1, head_count, head_size)
    gate_proj = projected[:, 3 * width:]
    scores = jnp.einsum('jhd,khd->hjk', query_proj, key_proj, precision=lax.Precision.HIGHEST)
    scores = scores + bias_plane + ((mask_row - 1.0) * 1000000000.0)[None, None, :]
    attention = jax.nn.softmax(scores, axis=-1)
    mixed_out = jnp.einsum('hjk,khd->jhd', attention, value_proj, precision=lax.Precision.HIGHEST).reshape(-1, width)
    return jnp.dot(jax.nn.sigmoid(gate_proj) * mixed_out, w_out, precision=lax.Precision.HIGHEST)

def start_attention(pair_in, mask_float, same_chain, scales, w_proj, w_bias, w_out, chain_row):
    normed = layer_norm(pair_in, scales)
    bias_plane = jnp.einsum('jkc,ch->hjk', normed, w_bias, precision=lax.Precision.HIGHEST)
    bias_plane = bias_plane + chain_row[:, None, None] * same_chain[None]
    update = lax.map(lambda inputs: attend_row(inputs[0], inputs[1], bias_plane, w_proj, w_out), (normed, mask_float))
    return pair_in + update

def reference(pair_state, pair_mask, chain_ids, ln_gain, w_proj, w_bias, w_out, chain_gain):
    mask_float = pair_mask.astype(jnp.float32)
    same_chain = (chain_ids[:, None] == chain_ids[None, :]).astype(jnp.float32)
    first_pair = start_attention(pair_state, mask_float, same_chain, ln_gain[0], w_proj[0], w_bias[0], w_out[0], chain_gain[0])
    turned = jnp.transpose(first_pair, (1, 0, 2))
    second = start_attention(turned, mask_float.T, same_chain, ln_gain[1], w_proj[1], w_bias[1], w_out[1], chain_gain[1])
    return jnp.transpose(second, (1, 0, 2))
```

```python
import functools
import jax
import jax.numpy as jnp
from jax import lax
from jax.experimental import pallas as pl
from jax.experimental.pallas import tpu as pltpu
from jax.sharding import Mesh, PartitionSpec as P

N = 768
HEADS = 4
LINES = 6
SLOT = 40
LOG2E = 1.4426950408889634
F32 = jnp.float32
BF16 = jnp.bfloat16
ROW = ("z", "x_hi", "core")
COL = ("y", "x_lo")
EVERY = ROW + COL
GATHER = ("z", "x_hi", "x_lo", "y", "core")
NT = (((1,), (1,)), ((), ()))
TN = (((0,), (0,)), ((), ()))


def split(values):
    high = values.astype(BF16)
    return high, (values - high.astype(F32)).astype(BF16)


def layer_norm(values, scales):
    average = jnp.mean(values, axis=-1, keepdims=True)
    centred = values - average
    variance = jnp.mean(centred * centred, axis=-1, keepdims=True)
    return centred * lax.rsqrt(variance + 1e-05) * scales


def halves(values):
    return values[:, :128] + values[:, 128:]


def gathered_place(row, col):
    return (row // 2) * 16 + (col % 2) * 8 + (col // 2) * 2 + row % 2


def order_bias(gathered, bias, keys_by_col):
    def step(outer, _):
        for part in range(4):
            if keys_by_col:
                owners = [gathered_place(part * 4 + t, outer) for t in range(4)]
            else:
                owners = [gathered_place(outer * 2 + part // 2, (part % 2) * 4 + t) for t in range(4)]
            blocks = [
                gathered[pl.ds(pl.multiple_of(owner * 24, 8), 24), :] for owner in owners
            ]
            start = pl.multiple_of(outer * 96 + part * 24, 8)
            for head in range(HEADS):
                rows = [block[head * LINES : (head + 1) * LINES] for block in blocks]
                bias[head, pl.ds(start, 24), :] = jnp.concatenate(rows, axis=0)
        return 0

    lax.fori_loop(0, 8, step, 0)


def attend(x, mask, bias, w_query, w_key, w_value, w_gate, w_out, gain, query, key, value, mixed, gate):
    normed_high, normed_low = split(layer_norm(x, gain))
    normed = jnp.concatenate([normed_high, normed_low], axis=1)

    def turned(weights):
        both = lax.dot_general(weights[...], normed, NT, preferred_element_type=F32)
        return both[:128] + both[128:]

    key_proj = halves(jnp.dot(normed, w_key[...], preferred_element_type=F32))
    query_high, query_low = split(turned(w_query))
    value_high, value_low = split(turned(w_value))
    gate[...] = turned(w_gate)
    block = lax.broadcasted_iota(jnp.int32, (1, 128), 1) // 32
    masked = jnp.broadcast_to(mask - 1.0, (N, 128))
    key_high = key_proj.astype(BF16).astype(F32)
    key_low = pltpu.roll(key_proj - key_high, 64, 1)
    key_again = pltpu.roll(key_high, 32, 1)
    place = lax.broadcasted_iota(jnp.int32, (32, N), 0)
    weight = jnp.where(
        place == 0, 1442840576.0, jnp.where(place == 1, -145408.0, jnp.where(place == 2, -128.0, 0.0))
    ).astype(BF16)
    ones = jnp.ones((16, N), BF16)
    for head in range(HEADS):
        at = [(head + t) % 4 for t in range(4)]
        part = slice(head * 32, (head + 1) * 32)
        key[head] = jnp.where(
            block == at[0],
            key_high,
            jnp.where(block == at[1], key_again, jnp.where(block == at[2], key_low, masked)),
        ).astype(BF16)
        rows = [None] * 4
        rows[at[0]] = query_high[part]
        rows[at[1]] = query_low[part]
        rows[at[2]] = query_high[part]
        rows[at[3]] = weight
        query[head] = jnp.concatenate(rows, axis=0)
        value[head] = jnp.concatenate([value_high[part], value_low[part], ones], axis=0)
    width = 256
    for head in range(HEADS):
        for start in range(0, N, width):
            span = slice(start, start + width)
            scores = jnp.dot(key[head], query[head, :, span], preferred_element_type=F32)
            scores = scores + bias[head, :, span]
            weights = jnp.exp2(scores - jnp.max(scores, axis=0, keepdims=True))
            high, low = split(weights)
            total = jnp.dot(value[head], high, preferred_element_type=F32)
            total = total + jnp.dot(value[head], low, preferred_element_type=F32)
            mixed[head * 32 : (head + 1) * 32, span] = (total[:32] + total[32:64]) / total[64:65]
    gated_high, gated_low = split(jax.nn.sigmoid(gate[...]) * mixed[...])
    gated = jnp.concatenate([gated_high, gated_low], axis=0)
    return halves(lax.dot_general(gated, w_out[...], TN, preferred_element_type=F32))


def start_kernel(
    x_ref, mask_ref, gathered, w_query, w_key, w_value, w_gate, w_out, gain, end_gain, w_bias, chain, same,
    pair_ref, bias_ref, bias, query, key, value, mixed, gate, line,
):
    step = pl.program_id(0)

    @pl.when(step == 0)
    def _():
        order_bias(gathered, bias, True)
        pair_ref[...] = jnp.zeros_like(pair_ref)

    x = x_ref[...].reshape(N, 128)
    update = attend(
        x, mask_ref[0], bias, w_query, w_key, w_value, w_gate, w_out, gain[...], query, key, value, mixed, gate
    )
    first = x + update
    line[...] = first
    for row in range(16):
        for t in range(LINES):
            pair_ref[pl.ds(row * 8 * SLOT + step * LINES + t, 8, stride=SLOT), :] = line[
                pl.ds(row * LINES + t, 8, stride=96), :
            ]
    normed = layer_norm(first, end_gain[...])
    plane = lax.dot_general(
        w_bias[...], normed, NT, precision=lax.Precision.HIGHEST, preferred_element_type=F32
    )
    plane = (plane + chain[:, :1] * same[0]) * LOG2E
    for head in range(HEADS):
        bias_ref[pl.ds(head * LINES + step, 1), :] = plane[head : head + 1]


def end_kernel(
    x_ref, mask_ref, gathered, w_query, w_key, w_value, w_gate, w_out, gain,
    out_ref, bias, query, key, value, mixed, gate, line,
):
    step = pl.program_id(0)

    @pl.when(step == 0)
    def _():
        order_bias(gathered, bias, False)

    for t in range(LINES):
        for group in range(16):
            line[pl.ds(group * 8 * LINES + t, 8, stride=LINES), :] = x_ref[
                pl.ds(group * 8 * SLOT + t * LINES + step, 8, stride=SLOT), :
            ]
    x = line[...]
    update = attend(
        x, mask_ref[0], bias, w_query, w_key, w_value, w_gate, w_out, gain[...], query, key, value, mixed, gate
    )
    out_ref[...] = (x + update).reshape(16, 1, 48, 128)


def whole(shape):
    return pl.BlockSpec(shape, lambda i: (0,) * len(shape), pipeline_mode=pl.Buffered(1))


SCRATCH = [
    pltpu.VMEM((HEADS, N, N), F32),
    pltpu.VMEM((HEADS, 128, N), BF16),
    pltpu.VMEM((HEADS, N, 128), BF16),
    pltpu.VMEM((HEADS, 80, N), BF16),
    pltpu.VMEM((128, N), F32),
    pltpu.VMEM((128, N), F32),
    pltpu.VMEM((N, 128), F32),
]
PARAMS = pltpu.CompilerParams(vmem_limit_bytes=56 * 1024 * 1024)


def doubled(weights):
    high = lax.reduce_precision(weights, 8, 7)
    both = jnp.concatenate([high, weights - high], axis=1)
    return jnp.concatenate([both, both], axis=0).astype(BF16)


def prepared(w_proj, w_out):
    w_query = doubled(w_proj[:, :128] * (32 ** -0.5 * LOG2E)).T
    w_key = doubled(w_proj[:, 128:256])
    w_value = doubled(w_proj[:, 256:384]).T
    w_gate = doubled(w_proj[:, 384:]).T
    return w_query, w_key, w_value, w_gate, doubled(w_out)


def local(pair_state, pair_mask, chain_ids, ln_gain, w_proj, w_bias, w_out, chain_gain):
    row, col = lax.axis_index(ROW), lax.axis_index(COL)
    mask_float = pair_mask.astype(F32)
    rows_pair = lax.all_to_all(pair_state, COL, split_axis=0, concat_axis=0, tiled=True)
    rows_pair = rows_pair.reshape(8, LINES, 96, 128)
    rows_mask = lax.all_to_all(mask_float, COL, split_axis=0, concat_axis=0, tiled=True)
    rows_mask = jnp.transpose(rows_mask.reshape(8, LINES, 96), (1, 0, 2)).reshape(LINES, N, 1)

    normed = layer_norm(pair_state, ln_gain[0])
    tile_bias = jnp.einsum("jkc,ch->hjk", normed, w_bias[0], precision=lax.Precision.HIGHEST)
    ids_row = lax.dynamic_slice(chain_ids, (row * 48,), (48,))
    ids_col = lax.dynamic_slice(chain_ids, (col * 96,), (96,))
    same = (ids_row[:, None] == ids_col[None, :]).astype(F32)
    tile_bias = (tile_bias + chain_gain[0][:, None, None] * same[None]) * LOG2E
    planes = jnp.concatenate([tile_bias, mask_float[None]], axis=0)
    planes = jnp.transpose(planes.reshape(5, 48, 16, LINES), (2, 0, 3, 1))
    planes = lax.all_to_all(planes, ROW, split_axis=0, concat_axis=0, tiled=True)
    planes = jnp.transpose(planes, (1, 2, 0, 3)).reshape(5, LINES, N)
    ends_mask = planes[4].reshape(LINES, N, 1)
    start_bias = lax.all_gather(planes[:4].reshape(24, N), GATHER, axis=0, tiled=True)

    ids_line = lax.dynamic_slice(chain_ids, (row * 48 + col * LINES,), (LINES,))
    same_line = (ids_line[:, None] == chain_ids[None, :]).astype(F32).reshape(LINES, 1, N)
    end_w = jnp.concatenate([w_bias[1].T, jnp.zeros((4, 128), F32)], axis=0)
    chain = jnp.broadcast_to(jnp.concatenate([chain_gain[1], jnp.zeros((4,), F32)])[:, None], (8, 128))
    matrix = whole((256, 256))
    first_pair, end_shard = pl.pallas_call(
        start_kernel,
        grid=(LINES,),
        out_shape=(
            jax.ShapeDtypeStruct((128 * SLOT, 128), F32),
            jax.ShapeDtypeStruct((HEADS * LINES, N), F32),
        ),
        in_specs=[
            pl.BlockSpec((8, 1, 96, 128), lambda i: (0, i, 0, 0)),
            pl.BlockSpec((1, N, 1), lambda i: (i, 0, 0)),
            whole((128 * 24, N)),
            matrix, matrix, matrix, matrix, matrix,
            whole((1, 128)), whole((1, 128)), whole((8, 128)), whole((8, 128)),
            pl.BlockSpec((1, 1, N), lambda i: (i, 0, 0)),
        ],
        out_specs=(whole((128 * SLOT, 128)), whole((HEADS * LINES, N))),
        scratch_shapes=SCRATCH,
        compiler_params=PARAMS,
        name="start_attention",
    )(
        rows_pair, rows_mask, start_bias, *prepared(w_proj[0], w_out[0]),
        ln_gain[0:1], ln_gain[1:2], end_w, chain, same_line,
    )
    end_bias = lax.all_gather(end_shard, GATHER, axis=0, tiled=True)
    columns = lax.all_to_all(
        first_pair.reshape(128, SLOT, 128), EVERY, split_axis=0, concat_axis=0, tiled=True
    ).reshape(128 * SLOT, 128)
    second = pl.pallas_call(
        end_kernel,
        grid=(LINES,),
        out_shape=jax.ShapeDtypeStruct((16, LINES, 48, 128), F32),
        in_specs=[
            whole((128 * SLOT, 128)),
            pl.BlockSpec((1, N, 1), lambda i: (i, 0, 0)),
            whole((128 * 24, N)),
            matrix, matrix, matrix, matrix, matrix,
            whole((1, 128)),
        ],
        out_specs=pl.BlockSpec((16, 1, 48, 128), lambda i: (0, i, 0, 0)),
        scratch_shapes=SCRATCH,
        compiler_params=PARAMS,
        name="end_attention",
    )(columns, ends_mask, end_bias, *prepared(w_proj[1], w_out[1]), ln_gain[1:2])
    returned = lax.all_to_all(second, ROW, split_axis=0, concat_axis=0, tiled=True)
    return jnp.transpose(returned, (2, 0, 1, 3)).reshape(48, 96, 128)


def solution(mesh):
    parts = Mesh(mesh.devices.reshape(4, 2, 2, 4, 2), ("z", "x_hi", "core", "y", "x_lo"))
    return jax.shard_map(
        local,
        mesh=parts,
        in_specs=(P(ROW, COL, None), P(ROW, COL), P(), P(), P(), P(), P(), P()),
        out_specs=P(ROW, COL, None),
        check_vma=False,
    )
```

```python
import functools
import jax
import jax.numpy as jnp
from jax import lax
from jax.experimental import pallas as pl
from jax.experimental.pallas import tpu as pltpu
from jax.sharding import Mesh, PartitionSpec as P

N = 768
HEADS = 4
LINES = 6
SLOT = 40
LOG2E = 1.4426950408889634
F32 = jnp.float32
BF16 = jnp.bfloat16
ROW = ("z", "x_hi", "core")
COL = ("y", "x_lo")
EVERY = ROW + COL
GATHER = ("z", "x_hi", "x_lo", "y", "core")
NT = (((1,), (1,)), ((), ()))
TN = (((0,), (0,)), ((), ()))


def split(values):
    high = values.astype(BF16)
    return high, (values - high.astype(F32)).astype(BF16)


def layer_norm(values, scales):
    average = jnp.mean(values, axis=-1, keepdims=True)
    centred = values - average
    variance = jnp.mean(centred * centred, axis=-1, keepdims=True)
    return centred * lax.rsqrt(variance + 1e-05) * scales


def halves(values):
    return values[:, :128] + values[:, 128:]


def gathered_place(row, col):
    return (row // 2) * 16 + (col % 2) * 8 + (col // 2) * 2 + row % 2


def order_tiles(gathered, bias):
    slot = lax.broadcasted_iota(jnp.int32, (1, 128), 1) // 16

    def step(col, _):
        for tile in range(6):
            pieces = []
            for t in range(8):
                row, part = divmod(tile * 8 + t, 3)
                start = pl.multiple_of(gathered_place(row, col) * 144 + part * 48, 8)
                pieces.append(gathered[pl.ds(start, 48), :])
            for distance in (4, 2, 1):
                upper = (slot // distance) % 2 == 1
                moved = list(pieces)
                for t in range(8):
                    if (t // distance) % 2 == 0:
                        one, two = pieces[t], pieces[t + distance]
                        moved[t] = jnp.where(upper, pltpu.roll(two, 16 * distance, 1), one)
                        moved[t + distance] = jnp.where(upper, two, pltpu.roll(one, 128 - 16 * distance, 1))
                pieces = moved
            for t in range(8):
                start = pl.multiple_of(col * 96 + (t // 4) * 48, 8)
                bias[t % 4, pl.ds(start, 48), tile * 128 : (tile + 1) * 128] = pieces[t]
        return 0

    lax.fori_loop(0, 8, step, 0)


def order_lines(gathered, bias):
    def step(outer, _):
        for part in range(4):
            owners = [gathered_place(outer * 2 + part // 2, (part % 2) * 4 + t) for t in range(4)]
            blocks = [gathered[pl.ds(pl.multiple_of(owner * 24, 8), 24), :] for owner in owners]
            start = pl.multiple_of(outer * 96 + part * 24, 8)
            for head in range(HEADS):
                rows = [block[head * LINES : (head + 1) * LINES] for block in blocks]
                bias[head, pl.ds(start, 24), :] = jnp.concatenate(rows, axis=0)
        return 0

    lax.fori_loop(0, 8, step, 0)


def tile_kernel(pair_ref, gain, w_lanes, chain, out_ref, normed):
    normed[...] = layer_norm(pair_ref[...].reshape(48 * 96, 128), gain[...])
    lane = lax.broadcasted_iota(jnp.int32, (128, 128), 1)
    total = chain[...]
    for t in range(16):
        rows = []
        for part in range(3):
            start = (part * 16 + t) * 96
            rows.append(jnp.concatenate([normed[start : start + 48, :], normed[start + 48 : start + 96, :]], axis=1))
        here = lane % 16 == t
        weights = jnp.concatenate(
            [jnp.where(here & (lane < 64), w_lanes[...], 0.0), jnp.where(here & (lane >= 64), w_lanes[...], 0.0)], axis=0
        )
        total = total + jnp.dot(
            jnp.concatenate(rows, axis=0), weights, precision=lax.Precision.HIGHEST, preferred_element_type=F32
        )
    out_ref[...] = total


def project(x, mask, w_query, w_key, w_value, w_gate, gain, query, key, value, gate):
    normed_high, normed_low = split(layer_norm(x, gain))
    normed = jnp.concatenate([normed_high, normed_low], axis=1)

    def turned(weights):
        both = lax.dot_general(weights[...], normed, NT, preferred_element_type=F32)
        return both[:128] + both[128:]

    key_proj = halves(jnp.dot(normed, w_key[...], preferred_element_type=F32))
    query_high, query_low = split(turned(w_query))
    value_high, value_low = split(turned(w_value))
    gate[0] = jax.nn.sigmoid(turned(w_gate))
    block = lax.broadcasted_iota(jnp.int32, (1, 128), 1) // 32
    masked = jnp.broadcast_to(mask - 1.0, (N, 128))
    key_high = key_proj.astype(BF16).astype(F32)
    key_low = pltpu.roll(key_proj - key_high, 64, 1)
    key_again = pltpu.roll(key_high, 32, 1)
    place = lax.broadcasted_iota(jnp.int32, (32, N), 0)
    weight = jnp.where(
        place == 0, 1442840576.0, jnp.where(place == 1, -145408.0, jnp.where(place == 2, -128.0, 0.0))
    ).astype(BF16)
    ones = jnp.ones((16, N), BF16)
    for head in range(HEADS):
        at = [(head + t) % 4 for t in range(4)]
        part = slice(head * 32, (head + 1) * 32)
        key[0, head] = jnp.where(
            block == at[0],
            key_high,
            jnp.where(block == at[1], key_again, jnp.where(block == at[2], key_low, masked)),
        ).astype(BF16)
        rows = [None] * 4
        rows[at[0]] = query_high[part]
        rows[at[1]] = query_low[part]
        rows[at[2]] = query_high[part]
        rows[at[3]] = weight
        query[0, head] = jnp.concatenate(rows, axis=0)
        value[0, head] = jnp.concatenate([value_high[part], value_low[part], ones], axis=0)


def attend(query, key, value, gate, bias, w_out, mixed):
    width = 256
    for head in range(HEADS):
        for start in range(0, N, width):
            span = slice(start, start + width)
            scores = jnp.dot(key[0, head], query[0, head, :, span], preferred_element_type=F32)
            scores = scores + bias[head, :, span]
            weights = jnp.exp2(scores - jnp.max(scores, axis=0, keepdims=True))
            high, low = split(weights)
            total = jnp.dot(value[0, head], high, preferred_element_type=F32)
            total = total + jnp.dot(value[0, head], low, preferred_element_type=F32)
            mixed[head * 32 : (head + 1) * 32, span] = (total[:32] + total[32:64]) / total[64:65]
    gated_high, gated_low = split(gate[0] * mixed[...])
    gated = jnp.concatenate([gated_high, gated_low], axis=0)
    return halves(lax.dot_general(gated, w_out[...], TN, preferred_element_type=F32))


def start_project_kernel(x_ref, mask_ref, w_query, w_key, w_value, w_gate, gain, query, key, value, gate):
    x = x_ref[...].reshape(N, 128)
    project(x, mask_ref[0], w_query, w_key, w_value, w_gate, gain[...], query, key, value, gate)


def end_project_kernel(x_ref, mask_ref, w_query, w_key, w_value, w_gate, gain, query, key, value, gate, line_ref, line):
    step = pl.program_id(0)
    for t in range(LINES):
        for group in range(16):
            line[pl.ds(group * 8 * LINES + t, 8, stride=LINES), :] = x_ref[
                pl.ds(group * 8 * SLOT + t * LINES + step, 8, stride=SLOT), :
            ]
    x = line[...]
    line_ref[0] = x
    project(x, mask_ref[0], w_query, w_key, w_value, w_gate, gain[...], query, key, value, gate)


def start_kernel(
    x_ref, query, key, value, gate, gathered, w_out, end_gain, w_bias, chain, same, pair_ref, bias_ref, bias, mixed, line
):
    step = pl.program_id(0)

    @pl.when(step == 0)
    def _():
        order_tiles(gathered, bias)
        pair_ref[...] = jnp.zeros_like(pair_ref)

    first = x_ref[...].reshape(N, 128) + attend(query, key, value, gate, bias, w_out, mixed)
    line[...] = first
    for row in range(16):
        for t in range(LINES):
            pair_ref[pl.ds(row * 8 * SLOT + step * LINES + t, 8, stride=SLOT), :] = line[
                pl.ds(row * LINES + t, 8, stride=96), :
            ]
    normed = layer_norm(first, end_gain[...])
    plane = lax.dot_general(
        w_bias[...], normed, NT, precision=lax.Precision.HIGHEST, preferred_element_type=F32
    )
    plane = (plane + chain[:, :1] * same[0]) * LOG2E
    for head in range(HEADS):
        bias_ref[pl.ds(head * LINES + step, 1), :] = plane[head : head + 1]


def end_kernel(x_ref, query, key, value, gate, gathered, w_out, out_ref, bias, mixed):
    @pl.when(pl.program_id(0) == 0)
    def _():
        order_lines(gathered, bias)

    update = attend(query, key, value, gate, bias, w_out, mixed)
    out_ref[...] = (x_ref[0] + update).reshape(16, 1, 48, 128)


def whole(shape):
    return pl.BlockSpec(shape, lambda i: (0,) * len(shape), pipeline_mode=pl.Buffered(1))


def lines(*shape):
    return pl.BlockSpec((1, *shape), lambda i: (i,) + (0,) * len(shape))


MATRIX = whole((256, 256))
PROJECTED = [lines(HEADS, 128, N), lines(HEADS, N, 128), lines(HEADS, 80, N), lines(128, N)]
PROJECTED_SHAPES = [
    jax.ShapeDtypeStruct((LINES, HEADS, 128, N), BF16),
    jax.ShapeDtypeStruct((LINES, HEADS, N, 128), BF16),
    jax.ShapeDtypeStruct((LINES, HEADS, 80, N), BF16),
    jax.ShapeDtypeStruct((LINES, 128, N), F32),
]
PARAMS = pltpu.CompilerParams(vmem_limit_bytes=56 * 1024 * 1024)


def doubled(weights):
    high = lax.reduce_precision(weights, 8, 7)
    both = jnp.concatenate([high, weights - high], axis=1)
    return jnp.concatenate([both, both], axis=0).astype(BF16)


def prepared(w_proj, w_out):
    w_query = doubled(w_proj[:, :128] * (32 ** -0.5 * LOG2E)).T
    w_key = doubled(w_proj[:, 128:256])
    w_value = doubled(w_proj[:, 256:384]).T
    w_gate = doubled(w_proj[:, 384:]).T
    return w_query, w_key, w_value, w_gate, doubled(w_out)


def local(pair_state, pair_mask, chain_ids, ln_gain, w_proj, w_bias, w_out, chain_gain):
    row, col = lax.axis_index(ROW), lax.axis_index(COL)
    mask_float = pair_mask.astype(F32)
    ids_row = lax.dynamic_slice(chain_ids, (row * 48,), (48,)).reshape(3, 1, 1, 1, 16)
    ids_col = lax.dynamic_slice(chain_ids, (col * 96,), (96,)).reshape(2, 48).T.reshape(1, 48, 2, 1, 1)
    same = (ids_row == ids_col).astype(F32)
    tile_chain = (same * (chain_gain[0] * LOG2E).reshape(1, 1, 1, 4, 1)).reshape(144, 128)
    w_lanes = jnp.tile(jnp.repeat(w_bias[0] * LOG2E, 16, axis=1), (1, 2))
    tile_bias = pl.pallas_call(
        tile_kernel,
        out_shape=jax.ShapeDtypeStruct((144, 128), F32),
        scratch_shapes=[pltpu.VMEM((48 * 96, 128), F32)],
        compiler_params=PARAMS,
        name="tile_bias",
    )(pair_state, ln_gain[0:1], w_lanes, tile_chain)
    start_bias = lax.all_gather(tile_bias, GATHER, axis=0, tiled=True)

    rows_pair = lax.all_to_all(pair_state, COL, split_axis=0, concat_axis=0, tiled=True)
    rows_pair = rows_pair.reshape(8, LINES, 96, 128)
    rows_mask = lax.all_to_all(mask_float, COL, split_axis=0, concat_axis=0, tiled=True)
    rows_mask = jnp.transpose(rows_mask.reshape(8, LINES, 96), (1, 0, 2)).reshape(LINES, N, 1)
    ends_mask = jnp.transpose(mask_float.reshape(48, 16, LINES), (1, 2, 0))
    ends_mask = lax.all_to_all(ends_mask, ROW, split_axis=0, concat_axis=0, tiled=True)
    ends_mask = jnp.transpose(ends_mask, (1, 0, 2)).reshape(LINES, N, 1)

    *start_weights, start_out = prepared(w_proj[0], w_out[0])
    *end_weights, end_out = prepared(w_proj[1], w_out[1])
    row_block = pl.BlockSpec((8, 1, 96, 128), lambda i: (0, i, 0, 0))
    start_parts = pl.pallas_call(
        start_project_kernel,
        grid=(LINES,),
        out_shape=PROJECTED_SHAPES,
        in_specs=[row_block, lines(N, 1), MATRIX, MATRIX, MATRIX, MATRIX, whole((1, 128))],
        out_specs=PROJECTED,
        compiler_params=PARAMS,
        name="start_projections",
    )(rows_pair, rows_mask, *start_weights, ln_gain[0:1])

    ids_line = lax.dynamic_slice(chain_ids, (row * 48 + col * LINES,), (LINES,))
    same_line = (ids_line[:, None] == chain_ids[None, :]).astype(F32).reshape(LINES, 1, N)
    end_w = jnp.concatenate([w_bias[1].T, jnp.zeros((4, 128), F32)], axis=0)
    chain = jnp.broadcast_to(jnp.concatenate([chain_gain[1], jnp.zeros((4,), F32)])[:, None], (8, 128))
    first_pair, end_shard = pl.pallas_call(
        start_kernel,
        grid=(LINES,),
        out_shape=(
            jax.ShapeDtypeStruct((128 * SLOT, 128), F32),
            jax.ShapeDtypeStruct((HEADS * LINES, N), F32),
        ),
        in_specs=[
            row_block, *PROJECTED, whole((128 * 144, 128)), MATRIX,
            whole((1, 128)), whole((8, 128)), whole((8, 128)), lines(1, N),
        ],
        out_specs=(whole((128 * SLOT, 128)), whole((HEADS * LINES, N))),
        scratch_shapes=[pltpu.VMEM((HEADS, N, N), F32), pltpu.VMEM((128, N), F32), pltpu.VMEM((N, 128), F32)],
        compiler_params=PARAMS,
        name="start_attention",
    )(rows_pair, *start_parts, start_bias, start_out, ln_gain[1:2], end_w, chain, same_line)

    end_bias = lax.all_gather(end_shard, GATHER, axis=0, tiled=True)
    columns = lax.all_to_all(
        first_pair.reshape(128, SLOT, 128), EVERY, split_axis=0, concat_axis=0, tiled=True
    ).reshape(128 * SLOT, 128)
    *end_parts, end_lines = pl.pallas_call(
        end_project_kernel,
        grid=(LINES,),
        out_shape=PROJECTED_SHAPES + [jax.ShapeDtypeStruct((LINES, N, 128), F32)],
        in_specs=[whole((128 * SLOT, 128)), lines(N, 1), MATRIX, MATRIX, MATRIX, MATRIX, whole((1, 128))],
        out_specs=PROJECTED + [lines(N, 128)],
        scratch_shapes=[pltpu.VMEM((N, 128), F32)],
        compiler_params=PARAMS,
        name="end_projections",
    )(columns, ends_mask, *end_weights, ln_gain[1:2])
    second = pl.pallas_call(
        end_kernel,
        grid=(LINES,),
        out_shape=jax.ShapeDtypeStruct((16, LINES, 48, 128), F32),
        in_specs=[lines(N, 128), *PROJECTED, whole((128 * 24, N)), MATRIX],
        out_specs=pl.BlockSpec((16, 1, 48, 128), lambda i: (0, i, 0, 0)),
        scratch_shapes=[pltpu.VMEM((HEADS, N, N), F32), pltpu.VMEM((128, N), F32)],
        compiler_params=PARAMS,
        name="end_attention",
    )(end_lines, *end_parts, end_bias, end_out)
    returned = lax.all_to_all(second, ROW, split_axis=0, concat_axis=0, tiled=True)
    return jnp.transpose(returned, (2, 0, 1, 3)).reshape(48, 96, 128)


def solution(mesh):
    parts = Mesh(mesh.devices.reshape(4, 2, 2, 4, 2), ("z", "x_hi", "core", "y", "x_lo"))
    return jax.shard_map(
        local,
        mesh=parts,
        in_specs=(P(ROW, COL, None), P(ROW, COL), P(), P(), P(), P(), P(), P()),
        out_specs=P(ROW, COL, None),
        check_vma=False,
    )
```

```python
import functools
import jax
import jax.numpy as jnp
from jax import lax
from jax.experimental import pallas as pl
from jax.experimental.pallas import tpu as pltpu
from jax.sharding import Mesh, PartitionSpec as P

N = 768
HEADS = 4
LINES = 6
SLOT = 40
PART = 584
PAIR = 1
LOG2E = 1.4426950408889634
F32 = jnp.float32
BF16 = jnp.bfloat16
ROW = ("z", "x_hi", "core")
COL = ("y", "x_lo")
EVERY = ROW + COL
NT = (((1,), (1,)), ((), ()))
TN = (((0,), (0,)), ((), ()))


def split(values):
    high = values.astype(BF16)
    return high, (values - high.astype(F32)).astype(BF16)


def layer_norm(values, scales):
    average = jnp.mean(values, axis=-1, keepdims=True)
    centred = values - average
    variance = jnp.mean(centred * centred, axis=-1, keepdims=True)
    return centred * lax.rsqrt(variance + 1e-05) * scales


def halves(values):
    return values[:, :128] + values[:, 128:]


def start_place(row, col):
    ahead = lax.rem(col // 2 + 4 - lax.axis_index("y"), 4)
    along_y = jnp.where(ahead == 0, 0, jnp.where(ahead == 1, 2, jnp.where(ahead == 2, 3, 1)))
    return ((row // 2 * 2 + col % 2) * 2 + row % 2) * 4 + along_y


def gather_start(shard):
    received = [lax.ppermute(shard, "y", [(t, (t + hop) % 4) for t in range(4)]) for hop in (1, 3, 2)]
    blocks = jnp.concatenate([shard, *received], axis=0)
    return lax.all_gather(blocks, ("z", "x_hi", "x_lo", "core"), axis=0, tiled=True)


def end_place(row, col):
    return (row // 2) * 16 + (col % 2) * 8 + (col // 2) * 2 + row % 2


def gather_end(shard):
    return lax.all_gather(shard, ("z", "x_hi", "x_lo", "y", "core"), axis=0, tiled=True)


def order_tiles(gathered, bias):
    slot = lax.broadcasted_iota(jnp.int32, (1, 128), 1) // 16

    def step(col, _):
        for tile in range(6):
            pieces = []
            for t in range(8):
                row, part = divmod(tile * 8 + t, 3)
                start = pl.multiple_of(start_place(row, col) * 144 + part * 48, 8)
                pieces.append(gathered[pl.ds(start, 48), :])
            for distance in (4, 2, 1):
                upper = (slot // distance) % 2 == 1
                moved = list(pieces)
                for t in range(8):
                    if (t // distance) % 2 == 0:
                        one, two = pieces[t], pieces[t + distance]
                        moved[t] = jnp.where(upper, pltpu.roll(two, 16 * distance, 1), one)
                        moved[t + distance] = jnp.where(upper, two, pltpu.roll(one, 128 - 16 * distance, 1))
                pieces = moved
            for t in range(8):
                start = pl.multiple_of(col * 96 + (t // 4) * 48, 8)
                bias[t % 4, pl.ds(start, 48), tile * 128 : (tile + 1) * 128] = pieces[t]
        return 0

    lax.fori_loop(0, 8, step, 0)


def order_lines(gathered, bias):
    def step(outer, _):
        for part in range(4):
            owners = [end_place(outer * 2 + part // 2, (part % 2) * 4 + t) for t in range(4)]
            blocks = [gathered[pl.ds(pl.multiple_of(owner * 24, 8), 24), :] for owner in owners]
            start = pl.multiple_of(outer * 96 + part * 24, 8)
            for head in range(HEADS):
                rows = [block[head * LINES : (head + 1) * LINES] for block in blocks]
                bias[head, pl.ds(start, 24), :] = jnp.concatenate(rows, axis=0)
        return 0

    lax.fori_loop(0, 8, step, 0)


def tile_kernel(ids, chain_gain, pair_ref, mask_ref, gain, w_bias, out_ref, parts_ref, normed):
    mask = jnp.concatenate([mask_ref[...].astype(F32), jnp.zeros((48, 32), F32)], axis=1)
    for part in range(8):
        inside = slice(part * LINES, (part + 1) * LINES)
        parts_ref[part, : LINES * 96] = pair_ref[inside].reshape(LINES * 96, 128)
        parts_ref[part, LINES * 96 :] = jnp.concatenate([mask[inside], jnp.zeros((2, 128), F32)], axis=0)
    normed[...] = layer_norm(pair_ref[...].reshape(48 * 96, 128), gain[:1])
    lane = lax.broadcasted_iota(jnp.int32, (128, 128), 1)
    head = (lane // 16) % 4
    w_lanes = sum(jnp.where(head == t, w_bias[0][:, t : t + 1] * LOG2E, 0.0) for t in range(HEADS))
    first_row, first_col = lax.axis_index(ROW) * 48, lax.axis_index(COL) * 96
    wide = lane[:1]
    gains = sum(jnp.where(head[:1] == t, chain_gain[0, t] * LOG2E, 0.0) for t in range(HEADS))
    place = lax.broadcasted_iota(jnp.int32, (48, 128), 0)
    keys = jnp.zeros((48, 128), jnp.int32)
    for t in range(48):
        ends = jnp.where(wide < 64, ids[first_col + t], ids[first_col + 48 + t])
        keys = jnp.where(place == t, ends, keys)
    total = []
    for part in range(3):
        queries = sum(jnp.where(wide % 16 == t, ids[first_row + part * 16 + t], 0) for t in range(16))
        total.append(jnp.where(keys == queries, gains, 0.0))
    total = jnp.concatenate(total, axis=0)
    for t in range(16):
        rows = []
        for part in range(3):
            start = (part * 16 + t) * 96
            rows.append(jnp.concatenate([normed[start : start + 48, :], normed[start + 48 : start + 96, :]], axis=1))
        here = lane % 16 == t
        weights = jnp.concatenate(
            [jnp.where(here & (lane < 64), w_lanes, 0.0), jnp.where(here & (lane >= 64), w_lanes, 0.0)], axis=0
        )
        total = total + jnp.dot(
            jnp.concatenate(rows, axis=0), weights, precision=lax.Precision.HIGHEST, preferred_element_type=F32
        )
    out_ref[...] = total


def project(x, mask, w_query, w_key, w_value, w_gate, gain, query, key, value, gate):
    normed_high, normed_low = split(layer_norm(x, gain))
    normed = jnp.concatenate([normed_high, normed_low], axis=1)

    def turned(weights):
        both = lax.dot_general(weights[...], normed, NT, preferred_element_type=F32)
        return both[:128] + both[128:]

    key_proj = halves(jnp.dot(normed, w_key[...], preferred_element_type=F32))
    query_high, query_low = split(turned(w_query))
    value_high, value_low = split(turned(w_value))
    gate[0] = jax.nn.sigmoid(turned(w_gate))
    block = lax.broadcasted_iota(jnp.int32, (1, 128), 1) // 32
    masked = jnp.broadcast_to(mask - 1.0, (N, 128))
    key_high = key_proj.astype(BF16).astype(F32)
    key_low = pltpu.roll(key_proj - key_high, 64, 1)
    key_again = pltpu.roll(key_high, 32, 1)
    place = lax.broadcasted_iota(jnp.int32, (32, N), 0)
    weight = jnp.where(
        place == 0, 1442840576.0, jnp.where(place == 1, -145408.0, jnp.where(place == 2, -128.0, 0.0))
    ).astype(BF16)
    ones = jnp.ones((16, N), BF16)
    for head in range(HEADS):
        at = [(head + t) % 4 for t in range(4)]
        part = slice(head * 32, (head + 1) * 32)
        key[0, head] = jnp.where(
            block == at[0],
            key_high,
            jnp.where(block == at[1], key_again, jnp.where(block == at[2], key_low, masked)),
        ).astype(BF16)
        rows = [None] * 4
        rows[at[0]] = query_high[part]
        rows[at[1]] = query_low[part]
        rows[at[2]] = query_high[part]
        rows[at[3]] = weight
        query[0, head] = jnp.concatenate(rows, axis=0)
        value[0, head] = jnp.concatenate([value_high[part], value_low[part], ones], axis=0)


def attend(t, query, key, value, gate, bias, w_out, mixed):
    width = 256
    for head in range(HEADS):
        for start in range(0, N, width):
            span = slice(start, start + width)
            scores = jnp.dot(key[t, head], query[t, head, :, span], preferred_element_type=F32)
            scores = scores + bias[head, :, span]
            weights = jnp.exp2(scores - jnp.max(scores, axis=0, keepdims=True))
            high, low = split(weights)
            total = jnp.dot(value[t, head], high, preferred_element_type=F32)
            total = total + jnp.dot(value[t, head], low, preferred_element_type=F32)
            mixed[t, head * 32 : (head + 1) * 32, span] = (total[:32] + total[32:64]) / total[64:65]
    gated_high, gated_low = split(gate[t] * mixed[t])
    gated = jnp.concatenate([gated_high, gated_low], axis=0)
    return halves(lax.dot_general(gated, w_out[...], TN, preferred_element_type=F32))


def start_project_kernel(x_ref, mask_ref, w_query, w_key, w_value, w_gate, gain, query, key, value, gate):
    x = x_ref[...].reshape(N, 128)
    held = mask_ref[:, pl.ds(pl.program_id(0), 1), :].reshape(8, 128).T
    mask = jnp.concatenate([held[:96, part : part + 1] for part in range(8)], axis=0)
    project(x, mask, w_query, w_key, w_value, w_gate, gain[...], query, key, value, gate)


def end_project_kernel(x_ref, w_query, w_key, w_value, w_gate, gain, query, key, value, gate, line_ref, line, mask):
    step = pl.program_id(0)
    lane = lax.broadcasted_iota(jnp.int32, (1, 128), 1)
    for group in range(16):
        held = x_ref[pl.ds(group * 8 * SLOT + LINES * LINES, 8, stride=SLOT), :]
        for t in range(LINES):
            place = pl.ds(group * 8 * LINES + t, 8, stride=LINES)
            line[place, :] = x_ref[pl.ds(group * 8 * SLOT + t * LINES + step, 8, stride=SLOT), :]
            own = jnp.sum(jnp.where(lane == t * LINES + step, held, 0.0), axis=1, keepdims=True)
            mask[place, :] = jnp.broadcast_to(own, (8, 128))
    x = line[...]
    line_ref[0] = x
    project(x, mask[...], w_query, w_key, w_value, w_gate, gain[...], query, key, value, gate)


def start_kernel(
    x_ref, mask_ref, query, key, value, gate, gathered, w_out, end_gain, w_bias, chain, same, pair_ref, bias_ref, bias, mixed, line
):
    step = pl.program_id(0)

    @pl.when(step == 0)
    def _():
        order_tiles(gathered, bias)
        pair_ref[...] = jnp.zeros_like(pair_ref)
        for group in range(16):
            pair_ref[pl.ds(group * 8 * SLOT + LINES * LINES, 8, stride=SLOT), :] = mask_ref[group * 8 : group * 8 + 8]

    for t in range(PAIR):
        first = x_ref[...].reshape(N, 128) + attend(t, query, key, value, gate, bias, w_out, mixed)
        line[t] = first
        here = step * PAIR + t
        for row in range(16):
            for k in range(LINES):
                pair_ref[pl.ds(row * 8 * SLOT + here * LINES + k, 8, stride=SLOT), :] = line[
                    t, pl.ds(row * LINES + k, 8, stride=96), :
                ]
        normed = layer_norm(first, end_gain[...])
        plane = lax.dot_general(
            w_bias[...], normed, NT, precision=lax.Precision.HIGHEST, preferred_element_type=F32
        )
        plane = (plane + chain[:, :1] * same[t]) * LOG2E
        for head in range(HEADS):
            bias_ref[pl.ds(head * LINES + here, 1), :] = plane[head : head + 1]


def end_kernel(x_ref, query, key, value, gate, gathered, w_out, out_ref, bias, mixed):
    @pl.when(pl.program_id(0) == 0)
    def _():
        order_lines(gathered, bias)

    for t in range(PAIR):
        update = attend(t, query, key, value, gate, bias, w_out, mixed)
        out_ref[:, t] = (x_ref[t] + update).reshape(16, 48, 128)


def whole(shape):
    return pl.BlockSpec(shape, lambda i: (0,) * len(shape), pipeline_mode=pl.Buffered(1))


def lines(*shape, count=1):
    return pl.BlockSpec((count, *shape), lambda i: (i,) + (0,) * len(shape))


def projected(count):
    shapes = [(HEADS, 128, N), (HEADS, N, 128), (HEADS, 80, N), (128, N)]
    return [lines(*shape, count=count) for shape in shapes]


MATRIX = whole((256, 256))
PROJECTED_SHAPES = [
    jax.ShapeDtypeStruct((LINES, HEADS, 128, N), BF16),
    jax.ShapeDtypeStruct((LINES, HEADS, N, 128), BF16),
    jax.ShapeDtypeStruct((LINES, HEADS, 80, N), BF16),
    jax.ShapeDtypeStruct((LINES, 128, N), F32),
]
PARAMS = pltpu.CompilerParams(vmem_limit_bytes=56 * 1024 * 1024)


def doubled(weights):
    high = lax.reduce_precision(weights, 8, 7)
    both = jnp.concatenate([high, weights - high], axis=1)
    return jnp.concatenate([both, both], axis=0).astype(BF16)


def prepared(w_proj, w_out):
    w_query = doubled(w_proj[:, :128] * (32 ** -0.5 * LOG2E)).T
    w_key = doubled(w_proj[:, 128:256])
    w_value = doubled(w_proj[:, 256:384]).T
    w_gate = doubled(w_proj[:, 384:]).T
    return w_query, w_key, w_value, w_gate, doubled(w_out)


def local(pair_state, pair_mask, chain_ids, ln_gain, w_proj, w_bias, w_out, chain_gain):
    row, col = lax.axis_index(ROW), lax.axis_index(COL)
    tile_bias, parts = pl.pallas_call(
        tile_kernel,
        out_shape=(jax.ShapeDtypeStruct((144, 128), F32), jax.ShapeDtypeStruct((8, PART, 128), F32)),
        in_specs=[
            pl.BlockSpec(memory_space=pltpu.SMEM),
            pl.BlockSpec(memory_space=pltpu.SMEM),
            pl.BlockSpec(memory_space=pltpu.VMEM),
            pl.BlockSpec(memory_space=pltpu.VMEM),
            pl.BlockSpec(memory_space=pltpu.VMEM),
            pl.BlockSpec(memory_space=pltpu.VMEM),
        ],
        scratch_shapes=[pltpu.VMEM((48 * 96, 128), F32)],
        compiler_params=PARAMS,
        name="tile_bias",
    )(chain_ids, chain_gain, pair_state, pair_mask, ln_gain, w_bias)
    start_bias = gather_start(tile_bias)

    rows = lax.all_to_all(parts, COL, split_axis=0, concat_axis=0, tiled=True)
    sent_mask = rows[:, LINES * 96 : LINES * 97, :96].reshape(8, LINES, 16, LINES)
    sent_mask = jnp.transpose(sent_mask, (2, 0, 1, 3)).reshape(128, LINES * LINES)
    sent_mask = jnp.pad(sent_mask, ((0, 0), (0, 128 - LINES * LINES)))

    *start_weights, start_out = prepared(w_proj[0], w_out[0])
    *end_weights, end_out = prepared(w_proj[1], w_out[1])
    row_block = pl.BlockSpec((8, 96, 128), lambda i: (0, i, 0))
    start_parts = pl.pallas_call(
        start_project_kernel,
        grid=(LINES,),
        out_shape=PROJECTED_SHAPES,
        in_specs=[row_block, pl.BlockSpec((8, 8, 128), lambda i: (0, 72, 0)), MATRIX, MATRIX, MATRIX, MATRIX, whole((1, 128))],
        out_specs=projected(1),
        compiler_params=PARAMS,
        name="start_projections",
    )(rows, rows, *start_weights, ln_gain[0:1])

    ids_line = lax.dynamic_slice(chain_ids, (row * 48 + col * LINES,), (LINES,))
    same_line = (ids_line[:, None] == chain_ids[None, :]).astype(F32).reshape(LINES, 1, N)
    end_w = jnp.concatenate([w_bias[1].T, jnp.zeros((4, 128), F32)], axis=0)
    chain = jnp.broadcast_to(jnp.concatenate([chain_gain[1], jnp.zeros((4,), F32)])[:, None], (8, 128))
    first_pair, end_shard = pl.pallas_call(
        start_kernel,
        grid=(LINES // PAIR,),
        out_shape=(
            jax.ShapeDtypeStruct((128 * SLOT, 128), F32),
            jax.ShapeDtypeStruct((HEADS * LINES, N), F32),
        ),
        in_specs=[
            row_block, whole((128, 128)),
            *projected(PAIR), whole((128 * 144, 128)), MATRIX,
            whole((1, 128)), whole((8, 128)), whole((8, 128)), lines(1, N, count=PAIR),
        ],
        out_specs=(whole((128 * SLOT, 128)), whole((HEADS * LINES, N))),
        scratch_shapes=[
            pltpu.VMEM((HEADS, N, N), F32),
            pltpu.VMEM((PAIR, 128, N), F32),
            pltpu.VMEM((PAIR, N, 128), F32),
        ],
        compiler_params=PARAMS,
        name="start_attention",
    )(rows, sent_mask, *start_parts, start_bias, start_out, ln_gain[1:2], end_w, chain, same_line)

    end_bias = gather_end(end_shard)
    columns = lax.all_to_all(
        first_pair.reshape(128, SLOT, 128), EVERY, split_axis=0, concat_axis=0, tiled=True
    ).reshape(128 * SLOT, 128)
    *end_parts, end_lines = pl.pallas_call(
        end_project_kernel,
        grid=(LINES,),
        out_shape=PROJECTED_SHAPES + [jax.ShapeDtypeStruct((LINES, N, 128), F32)],
        in_specs=[whole((128 * SLOT, 128)), MATRIX, MATRIX, MATRIX, MATRIX, whole((1, 128))],
        out_specs=projected(1) + [lines(N, 128)],
        scratch_shapes=[pltpu.VMEM((N, 128), F32), pltpu.VMEM((N, 128), F32)],
        compiler_params=PARAMS,
        name="end_projections",
    )(columns, *end_weights, ln_gain[1:2])
    second = pl.pallas_call(
        end_kernel,
        grid=(LINES // PAIR,),
        out_shape=jax.ShapeDtypeStruct((16, LINES, 48, 128), F32),
        in_specs=[lines(N, 128, count=PAIR), *projected(PAIR), whole((128 * 24, N)), MATRIX],
        out_specs=pl.BlockSpec((16, PAIR, 48, 128), lambda i: (0, i, 0, 0)),
        scratch_shapes=[pltpu.VMEM((HEADS, N, N), F32), pltpu.VMEM((PAIR, 128, N), F32)],
        compiler_params=PARAMS,
        name="end_attention",
    )(end_lines, *end_parts, end_bias, end_out)
    returned = lax.all_to_all(second, ROW, split_axis=0, concat_axis=0, tiled=True)
    return jnp.transpose(returned, (2, 0, 1, 3)).reshape(48, 96, 128)


def solution(mesh):
    parts = Mesh(mesh.devices.reshape(4, 2, 2, 4, 2), ("z", "x_hi", "core", "y", "x_lo"))
    return jax.shard_map(
        local,
        mesh=parts,
        in_specs=(P(ROW, COL, None), P(ROW, COL), P(), P(), P(), P(), P(), P()),
        out_specs=P(ROW, COL, None),
        check_vma=False,
    )
```

```python
import functools
import jax
import jax.numpy as jnp
from jax import lax
from jax.experimental import pallas as pl
from jax.experimental.pallas import tpu as pltpu
from jax.sharding import Mesh, PartitionSpec as P

N = 768
HEADS = 4
LINES = 6
SLOT = 40
PART = 584
PAIR = 1
LOG2E = 1.4426950408889634
F32 = jnp.float32
BF16 = jnp.bfloat16
ROW = ("z", "x_hi", "core")
COL = ("y", "x_lo")
EVERY = ROW + COL
NT = (((1,), (1,)), ((), ()))
TN = (((0,), (0,)), ((), ()))


def split(values):
    high = values.astype(BF16)
    return high, (values - high.astype(F32)).astype(BF16)


def layer_norm(values, scales):
    average = jnp.mean(values, axis=-1, keepdims=True)
    centred = values - average
    variance = jnp.mean(centred * centred, axis=-1, keepdims=True)
    return centred * lax.rsqrt(variance + 1e-05) * scales


def halves(values):
    return values[:, :128] + values[:, 128:]


def start_place(row, col):
    ahead = lax.rem(col // 2 + 4 - lax.axis_index("y"), 4)
    along_y = jnp.where(ahead == 0, 0, jnp.where(ahead == 1, 2, jnp.where(ahead == 2, 3, 1)))
    return ((row // 2 * 2 + col % 2) * 2 + row % 2) * 4 + along_y


def gather_start(shard):
    received = [lax.ppermute(shard, "y", [(t, (t + hop) % 4) for t in range(4)]) for hop in (1, 3, 2)]
    blocks = jnp.concatenate([shard, *received], axis=0)
    return lax.all_gather(blocks, ("z", "x_hi", "x_lo", "core"), axis=0, tiled=True)


def end_place(row, col):
    return (row // 2) * 16 + (col % 2) * 8 + (col // 2) * 2 + row % 2


def gather_end(shard):
    return lax.all_gather(shard, ("z", "x_hi", "x_lo", "y", "core"), axis=0, tiled=True)


def fetch(gathered, held, sems):
    size = held.shape[0] // 8
    copies = []
    for t in range(8):
        inside = pl.ds(t * size, size)
        copies.append(pltpu.make_async_copy(gathered.at[inside], held.at[inside], sems.at[t]))
        copies[-1].start()
    return copies


def order_tiles(copies, held, bias):
    slot = lax.broadcasted_iota(jnp.int32, (1, 128), 1) // 16
    arrived = 0
    for tile in range(6):
        while arrived <= (tile * 8 + 7) // 3 // 2:
            copies[arrived].wait()
            arrived += 1

        def step(col, _):
            pieces = []
            for t in range(8):
                row, part = divmod(tile * 8 + t, 3)
                start = pl.multiple_of(start_place(row, col) * 144 + part * 48, 8)
                pieces.append(held[pl.ds(start, 48), :])
            for hop in (1, 2, 4):
                upper = (slot // hop) % 2 == 1
                pieces = [jnp.where(upper, pieces[(t + hop) % 8], pieces[t]) for t in range(8)]
            for t in range(8):
                start = pl.multiple_of(col * 96 + (t // 4) * 48, 8)
                turned = pieces[(8 - t) % 8]
                if t:
                    turned = pltpu.roll(turned, 128 - 16 * t, 1)
                bias[t % 4, pl.ds(start, 48), tile * 128 : (tile + 1) * 128] = turned
            return 0

        lax.fori_loop(0, 8, step, 0)


def order_lines(copies, held, bias):
    for outer in range(8):
        copies[outer].wait()
        for part in range(4):
            owners = [end_place(outer * 2 + part // 2, (part % 2) * 4 + t) for t in range(4)]
            blocks = [held[owner * 24 : owner * 24 + 24, :] for owner in owners]
            start = outer * 96 + part * 24
            for head in range(HEADS):
                rows = [block[head * LINES : (head + 1) * LINES] for block in blocks]
                bias[head, start : start + 24, :] = jnp.concatenate(rows, axis=0)


def tile_kernel(ids, chain_gain, pair_ref, mask_ref, gain, w_bias, out_ref, parts_ref, normed):
    mask = jnp.concatenate([mask_ref[...].astype(F32), jnp.zeros((48, 32), F32)], axis=1)
    for part in range(8):
        inside = slice(part * LINES, (part + 1) * LINES)
        parts_ref[part, : LINES * 96] = pair_ref[inside].reshape(LINES * 96, 128)
        parts_ref[part, LINES * 96 :] = jnp.concatenate([mask[inside], jnp.zeros((2, 128), F32)], axis=0)
    normed[...] = layer_norm(pair_ref[...].reshape(48 * 96, 128), gain[:1])
    lane = lax.broadcasted_iota(jnp.int32, (128, 128), 1)
    head = (lane // 16) % 4
    columns = jnp.concatenate([w_bias[0], w_bias[0]], axis=0).T
    w_lanes = sum(jnp.where(head == t, columns[:, t : t + 1] * LOG2E, 0.0) for t in range(HEADS))
    first_row, first_col = lax.axis_index(ROW) * 48, lax.axis_index(COL) * 96
    wide = lane[:1]
    gains = sum(jnp.where(head[:1] == t, chain_gain[0, t] * LOG2E, 0.0) for t in range(HEADS))
    place = lax.broadcasted_iota(jnp.int32, (48, 128), 0)
    keys = jnp.zeros((48, 128), jnp.int32)
    for t in range(48):
        ends = jnp.where(wide < 64, ids[first_col + t], ids[first_col + 48 + t])
        keys = jnp.where(place == t, ends, keys)
    total = []
    for part in range(3):
        queries = sum(jnp.where(wide % 16 == t, ids[first_row + part * 16 + t], 0) for t in range(16))
        total.append(jnp.where(keys == queries, gains, 0.0))
    total = jnp.concatenate(total, axis=0)
    for t in range(16):
        rows = []
        for part in range(3):
            start = (part * 16 + t) * 96
            rows.append(jnp.concatenate([normed[start : start + 48, :], normed[start + 48 : start + 96, :]], axis=1))
        here = lane % 16 == t
        weights = jnp.concatenate(
            [jnp.where(here & (lane < 64), w_lanes, 0.0), jnp.where(here & (lane >= 64), w_lanes, 0.0)], axis=0
        )
        total = total + jnp.dot(
            jnp.concatenate(rows, axis=0), weights, precision=lax.Precision.HIGHEST, preferred_element_type=F32
        )
    for part in range(3):
        before = lax.rem(lax.axis_index(ROW) * 3 + part, 8)
        out_ref[part * 48 : part * 48 + 48] = pltpu.roll(total[part * 48 : part * 48 + 48], before * 16, 1)


def project(x, mask, w_query, w_key, w_value, w_gate, gain, query, key, value, gate):
    normed_high, normed_low = split(layer_norm(x, gain))
    normed = jnp.concatenate([normed_high, normed_low], axis=1)

    def turned(weights):
        both = lax.dot_general(weights[...], normed, NT, preferred_element_type=F32)
        return both[:128] + both[128:]

    key_proj = halves(jnp.dot(normed, w_key[...], preferred_element_type=F32))
    query_high, query_low = split(turned(w_query))
    value_high, value_low = split(turned(w_value))
    gate[0] = jax.nn.sigmoid(turned(w_gate))
    block = lax.broadcasted_iota(jnp.int32, (1, 128), 1) // 32
    masked = jnp.broadcast_to(mask - 1.0, (N, 128))
    key_high = key_proj.astype(BF16).astype(F32)
    key_low = pltpu.roll(key_proj - key_high, 64, 1)
    key_again = pltpu.roll(key_high, 32, 1)
    place = lax.broadcasted_iota(jnp.int32, (32, N), 0)
    weight = jnp.where(
        place == 0, 1442840576.0, jnp.where(place == 1, -145408.0, jnp.where(place == 2, -128.0, 0.0))
    ).astype(BF16)
    ones = jnp.ones((16, N), BF16)
    for head in range(HEADS):
        at = [(head + t) % 4 for t in range(4)]
        part = slice(head * 32, (head + 1) * 32)
        key[0, head] = jnp.where(
            block == at[0],
            key_high,
            jnp.where(block == at[1], key_again, jnp.where(block == at[2], key_low, masked)),
        ).astype(BF16)
        rows = [None] * 4
        rows[at[0]] = query_high[part]
        rows[at[1]] = query_low[part]
        rows[at[2]] = query_high[part]
        rows[at[3]] = weight
        query[0, head] = jnp.concatenate(rows, axis=0)
        value[0, head] = jnp.concatenate([value_high[part], value_low[part], ones], axis=0)


def attend(t, query, key, value, gate, bias, w_out, mixed):
    width = 256
    for head in range(HEADS):
        for start in range(0, N, width):
            span = slice(start, start + width)
            scores = jnp.dot(key[t, head], query[t, head, :, span], preferred_element_type=F32)
            scores = scores + bias[head, :, span]
            weights = jnp.exp2(scores - jnp.max(scores, axis=0, keepdims=True))
            high, low = split(weights)
            total = jnp.dot(value[t, head], high, preferred_element_type=F32)
            total = total + jnp.dot(value[t, head], low, preferred_element_type=F32)
            mixed[t, head * 32 : (head + 1) * 32, span] = (total[:32] + total[32:64]) / total[64:65]
    gated_high, gated_low = split(gate[t] * mixed[t])
    gated = jnp.concatenate([gated_high, gated_low], axis=0)
    return halves(lax.dot_general(gated, w_out[...], TN, preferred_element_type=F32))


def start_project_kernel(x_ref, mask_ref, w_query, w_key, w_value, w_gate, gain, query, key, value, gate):
    x = x_ref[...].reshape(N, 128)
    held = mask_ref[:, pl.ds(pl.program_id(0), 1), :].reshape(8, 128).T
    mask = jnp.concatenate([held[:96, part : part + 1] for part in range(8)], axis=0)
    project(x, mask, w_query, w_key, w_value, w_gate, gain[...], query, key, value, gate)


def end_project_kernel(x_ref, w_query, w_key, w_value, w_gate, gain, query, key, value, gate, line_ref, line, mask):
    step = pl.program_id(0)
    lane = lax.broadcasted_iota(jnp.int32, (1, 128), 1)
    for group in range(16):
        held = x_ref[pl.ds(group * 8 * SLOT + LINES * LINES, 8, stride=SLOT), :]
        for t in range(LINES):
            place = pl.ds(group * 8 * LINES + t, 8, stride=LINES)
            line[place, :] = x_ref[pl.ds(group * 8 * SLOT + t * LINES + step, 8, stride=SLOT), :]
            own = jnp.sum(jnp.where(lane == t * LINES + step, held, 0.0), axis=1, keepdims=True)
            mask[place, :] = jnp.broadcast_to(own, (8, 128))
    x = line[...]
    line_ref[0] = x
    project(x, mask[...], w_query, w_key, w_value, w_gate, gain[...], query, key, value, gate)


def start_kernel(
    x_ref, mask_ref, query, key, value, gate, gathered, w_out, end_gain, w_bias, chain_gain, same,
    pair_ref, bias_ref, bias, mixed, line, held, sems,
):
    step = pl.program_id(0)

    @pl.when(step == 0)
    def _():
        copies = fetch(gathered, held, sems)
        pair_ref[...] = jnp.zeros_like(pair_ref)
        for group in range(16):
            pair_ref[pl.ds(group * 8 * SLOT + LINES * LINES, 8, stride=SLOT), :] = mask_ref[group * 8 : group * 8 + 8]
        order_tiles(copies, held, bias)

    place = lax.broadcasted_iota(jnp.int32, (8, 1), 0)
    chain = sum(jnp.where(place == t, chain_gain[1, t], 0.0) for t in range(HEADS))
    for t in range(PAIR):
        first = x_ref[...].reshape(N, 128) + attend(t, query, key, value, gate, bias, w_out, mixed)
        line[t] = first
        here = step * PAIR + t
        for row in range(16):
            for k in range(LINES):
                pair_ref[pl.ds(row * 8 * SLOT + here * LINES + k, 8, stride=SLOT), :] = line[
                    t, pl.ds(row * LINES + k, 8, stride=96), :
                ]
        normed = layer_norm(first, end_gain[...])
        plane = lax.dot_general(
            w_bias[...], normed, NT, precision=lax.Precision.HIGHEST, preferred_element_type=F32
        )
        plane = (plane + chain * same[t]) * LOG2E
        for head in range(HEADS):
            bias_ref[pl.ds(head * LINES + here, 1), :] = plane[head : head + 1]


def end_kernel(x_ref, query, key, value, gate, gathered, w_out, out_ref, bias, mixed, held, sems):
    @pl.when(pl.program_id(0) == 0)
    def _():
        order_lines(fetch(gathered, held, sems), held, bias)

    for t in range(PAIR):
        update = attend(t, query, key, value, gate, bias, w_out, mixed)
        out_ref[:, t] = (x_ref[t] + update).reshape(16, 48, 128)


def whole(shape):
    return pl.BlockSpec(shape, lambda i: (0,) * len(shape), pipeline_mode=pl.Buffered(1))


def lines(*shape, count=1):
    return pl.BlockSpec((count, *shape), lambda i: (i,) + (0,) * len(shape))


def projected(count):
    shapes = [(HEADS, 128, N), (HEADS, N, 128), (HEADS, 80, N), (128, N)]
    return [lines(*shape, count=count) for shape in shapes]


MATRIX = whole((256, 256))
PROJECTED_SHAPES = [
    jax.ShapeDtypeStruct((LINES, HEADS, 128, N), BF16),
    jax.ShapeDtypeStruct((LINES, HEADS, N, 128), BF16),
    jax.ShapeDtypeStruct((LINES, HEADS, 80, N), BF16),
    jax.ShapeDtypeStruct((LINES, 128, N), F32),
]
PARAMS = pltpu.CompilerParams(vmem_limit_bytes=56 * 1024 * 1024)


def doubled(weights):
    high = lax.reduce_precision(weights, 8, 7)
    both = jnp.concatenate([high, weights - high], axis=1)
    return jnp.concatenate([both, both], axis=0).astype(BF16)


def prepared(w_proj, w_out):
    w_query = doubled(w_proj[:, :128] * (32 ** -0.5 * LOG2E)).T
    w_key = doubled(w_proj[:, 128:256])
    w_value = doubled(w_proj[:, 256:384]).T
    w_gate = doubled(w_proj[:, 384:]).T
    return w_query, w_key, w_value, w_gate, doubled(w_out)


def local(pair_state, pair_mask, chain_ids, ln_gain, w_proj, w_bias, w_out, chain_gain):
    row, col = lax.axis_index(ROW), lax.axis_index(COL)
    tile_bias, parts = pl.pallas_call(
        tile_kernel,
        out_shape=(jax.ShapeDtypeStruct((144, 128), F32), jax.ShapeDtypeStruct((8, PART, 128), F32)),
        in_specs=[
            pl.BlockSpec(memory_space=pltpu.SMEM),
            pl.BlockSpec(memory_space=pltpu.SMEM),
            pl.BlockSpec(memory_space=pltpu.VMEM),
            pl.BlockSpec(memory_space=pltpu.VMEM),
            pl.BlockSpec(memory_space=pltpu.VMEM),
            pl.BlockSpec(memory_space=pltpu.VMEM),
        ],
        scratch_shapes=[pltpu.VMEM((48 * 96, 128), F32)],
        compiler_params=PARAMS,
        name="tile_bias",
    )(chain_ids, chain_gain, pair_state, pair_mask, ln_gain, jnp.swapaxes(w_bias, 1, 2))
    start_bias = gather_start(tile_bias)

    rows = lax.all_to_all(parts, COL, split_axis=0, concat_axis=0, tiled=True)
    sent_mask = rows[:, LINES * 96 : LINES * 97, :96].reshape(8, LINES, 16, LINES)
    sent_mask = jnp.transpose(sent_mask, (2, 0, 1, 3)).reshape(128, LINES * LINES)
    sent_mask = jnp.pad(sent_mask, ((0, 0), (0, 128 - LINES * LINES)))

    *start_weights, start_out = prepared(w_proj[0], w_out[0])
    *end_weights, end_out = prepared(w_proj[1], w_out[1])
    row_block = pl.BlockSpec((8, 96, 128), lambda i: (0, i, 0))
    start_parts = pl.pallas_call(
        start_project_kernel,
        grid=(LINES,),
        out_shape=PROJECTED_SHAPES,
        in_specs=[row_block, pl.BlockSpec((8, 8, 128), lambda i: (0, 72, 0)), MATRIX, MATRIX, MATRIX, MATRIX, whole((1, 128))],
        out_specs=projected(1),
        compiler_params=PARAMS,
        name="start_projections",
    )(rows, rows, *start_weights, ln_gain[0:1])

    ids_line = lax.dynamic_slice(chain_ids, (row * 48 + col * LINES,), (LINES,))
    same_line = (ids_line[:, None] == chain_ids[None, :]).astype(F32).reshape(LINES, 1, N)
    end_w = jnp.concatenate([w_bias[1].T, jnp.zeros((4, 128), F32)], axis=0)
    first_pair, end_shard = pl.pallas_call(
        start_kernel,
        grid=(LINES // PAIR,),
        out_shape=(
            jax.ShapeDtypeStruct((128 * SLOT, 128), F32),
            jax.ShapeDtypeStruct((HEADS * LINES, N), F32),
        ),
        in_specs=[
            row_block, whole((128, 128)),
            *projected(PAIR), pl.BlockSpec(memory_space=pl.ANY), MATRIX,
            whole((1, 128)), whole((8, 128)), pl.BlockSpec(memory_space=pltpu.SMEM), lines(1, N, count=PAIR),
        ],
        out_specs=(whole((128 * SLOT, 128)), whole((HEADS * LINES, N))),
        scratch_shapes=[
            pltpu.VMEM((HEADS, N, N), F32),
            pltpu.VMEM((PAIR, 128, N), F32),
            pltpu.VMEM((PAIR, N, 128), F32),
            pltpu.VMEM((128 * 144, 128), F32),
            pltpu.SemaphoreType.DMA((8,)),
        ],
        compiler_params=PARAMS,
        name="start_attention",
    )(rows, sent_mask, *start_parts, start_bias, start_out, ln_gain[1:2], end_w, chain_gain, same_line)

    end_bias = gather_end(end_shard)
    columns = lax.all_to_all(
        first_pair.reshape(128, SLOT, 128), EVERY, split_axis=0, concat_axis=0, tiled=True
    ).reshape(128 * SLOT, 128)
    *end_parts, end_lines = pl.pallas_call(
        end_project_kernel,
        grid=(LINES,),
        out_shape=PROJECTED_SHAPES + [jax.ShapeDtypeStruct((LINES, N, 128), F32)],
        in_specs=[whole((128 * SLOT, 128)), MATRIX, MATRIX, MATRIX, MATRIX, whole((1, 128))],
        out_specs=projected(1) + [lines(N, 128)],
        scratch_shapes=[pltpu.VMEM((N, 128), F32), pltpu.VMEM((N, 128), F32)],
        compiler_params=PARAMS,
        name="end_projections",
    )(columns, *end_weights, ln_gain[1:2])
    second = pl.pallas_call(
        end_kernel,
        grid=(LINES // PAIR,),
        out_shape=jax.ShapeDtypeStruct((16, LINES, 48, 128), F32),
        in_specs=[lines(N, 128, count=PAIR), *projected(PAIR), pl.BlockSpec(memory_space=pl.ANY), MATRIX],
        out_specs=pl.BlockSpec((16, PAIR, 48, 128), lambda i: (0, i, 0, 0)),
        scratch_shapes=[
            pltpu.VMEM((HEADS, N, N), F32),
            pltpu.VMEM((PAIR, 128, N), F32),
            pltpu.VMEM((128 * 24, N), F32),
            pltpu.SemaphoreType.DMA((8,)),
        ],
        compiler_params=PARAMS,
        name="end_attention",
    )(end_lines, *end_parts, end_bias, end_out)
    returned = lax.all_to_all(second, ROW, split_axis=0, concat_axis=0, tiled=True)
    return jnp.transpose(returned, (2, 0, 1, 3)).reshape(48, 96, 128)


def solution(mesh):
    parts = Mesh(mesh.devices.reshape(4, 2, 2, 4, 2), ("z", "x_hi", "core", "y", "x_lo"))
    return jax.shard_map(
        local,
        mesh=parts,
        in_specs=(P(ROW, COL, None), P(ROW, COL), P(), P(), P(), P(), P(), P()),
        out_specs=P(ROW, COL, None),
        check_vma=False,
    )
```

```python
import functools
import jax
import jax.numpy as jnp
from jax import lax
from jax.experimental import pallas as pl
from jax.experimental.pallas import tpu as pltpu
from jax.sharding import Mesh, PartitionSpec as P

N = 768
HEADS = 4
LINES = 6
SLOT = 40
PART = 584
PAIR = 1
LOG2E = 1.4426950408889634
F32 = jnp.float32
BF16 = jnp.bfloat16
ROW = ("z", "x_hi", "core")
COL = ("y", "x_lo")
EVERY = ROW + COL
NT = (((1,), (1,)), ((), ()))
TN = (((0,), (0,)), ((), ()))


def split(values):
    high = values.astype(BF16)
    return high, (values - high.astype(F32)).astype(BF16)


def layer_norm(values, scales):
    average = jnp.mean(values, axis=-1, keepdims=True)
    centred = values - average
    variance = jnp.mean(centred * centred, axis=-1, keepdims=True)
    return centred * lax.rsqrt(variance + 1e-05) * scales


def halves(values):
    return values[:, :128] + values[:, 128:]


def start_place(row, col):
    ahead = lax.rem(col // 2 + 4 - lax.axis_index("y"), 4)
    along_y = jnp.where(ahead == 0, 0, jnp.where(ahead == 1, 2, jnp.where(ahead == 2, 3, 1)))
    return ((row // 2 * 2 + col % 2) * 2 + row % 2) * 4 + along_y


def gather_start(shard):
    received = [lax.ppermute(shard, "y", [(t, (t + hop) % 4) for t in range(4)]) for hop in (1, 3, 2)]
    blocks = jnp.concatenate([shard, *received], axis=0)
    return lax.all_gather(blocks, ("z", "x_hi", "x_lo", "core"), axis=0, tiled=True)


def end_place(row, col):
    return (row // 2) * 16 + (col % 2) * 8 + (col // 2) * 2 + row % 2


def gather_end(shard):
    return lax.all_gather(shard, ("z", "x_hi", "x_lo", "y", "core"), axis=0, tiled=True)


def fetch(gathered, held, sems):
    size = held.shape[0] // 8
    copies = []
    for t in range(8):
        inside = pl.ds(t * size, size)
        copies.append(pltpu.make_async_copy(gathered.at[inside], held.at[inside], sems.at[t]))
        copies[-1].start()
    return copies


def order_tiles(copies, held, bias):
    slot = lax.broadcasted_iota(jnp.int32, (1, 128), 1) // 16
    arrived = 0
    for tile in range(6):
        while arrived <= (tile * 8 + 7) // 3 // 2:
            copies[arrived].wait()
            arrived += 1

        def step(col, _):
            pieces = []
            for t in range(8):
                row, part = divmod(tile * 8 + t, 3)
                start = pl.multiple_of(start_place(row, col) * 144 + part * 48, 8)
                pieces.append(held[pl.ds(start, 48), :])
            for hop in (1, 2, 4):
                upper = (slot // hop) % 2 == 1
                pieces = [jnp.where(upper, pieces[(t + hop) % 8], pieces[t]) for t in range(8)]
            for t in range(8):
                start = pl.multiple_of(col * 96 + (t // 4) * 48, 8)
                turned = pieces[(8 - t) % 8]
                if t:
                    turned = pltpu.roll(turned, 128 - 16 * t, 1)
                bias[t % 4, pl.ds(start, 48), tile * 128 : (tile + 1) * 128] = turned
            return 0

        lax.fori_loop(0, 8, step, 0)


def order_lines(copies, held, bias):
    for outer in range(8):
        copies[outer].wait()
        for part in range(4):
            owners = [end_place(outer * 2 + part // 2, (part % 2) * 4 + t) for t in range(4)]
            blocks = [held[owner * 24 : owner * 24 + 24, :] for owner in owners]
            start = outer * 96 + part * 24
            for head in range(HEADS):
                rows = [block[head * LINES : (head + 1) * LINES] for block in blocks]
                bias[head, start : start + 24, :] = jnp.concatenate(rows, axis=0)


def tile_kernel(ids, chain_gain, pair_ref, mask_ref, gain, w_bias, out_ref, parts_ref, normed):
    mask = jnp.concatenate([mask_ref[...].astype(F32), jnp.zeros((48, 32), F32)], axis=1)
    for part in range(8):
        inside = slice(part * LINES, (part + 1) * LINES)
        parts_ref[part, : LINES * 96] = pair_ref[inside].reshape(LINES * 96, 128)
        parts_ref[part, LINES * 96 :] = jnp.concatenate([mask[inside], jnp.zeros((2, 128), F32)], axis=0)
    normed[...] = layer_norm(pair_ref[...].reshape(48 * 96, 128), gain[:1])
    lane = lax.broadcasted_iota(jnp.int32, (128, 128), 1)
    head = (lane // 16) % 4
    columns = jnp.concatenate([w_bias[0], w_bias[0]], axis=0).T
    w_lanes = sum(jnp.where(head == t, columns[:, t : t + 1] * LOG2E, 0.0) for t in range(HEADS))
    first_row, first_col = lax.axis_index(ROW) * 48, lax.axis_index(COL) * 96
    wide = lane[:1]
    gains = sum(jnp.where(head[:1] == t, chain_gain[0, t] * LOG2E, 0.0) for t in range(HEADS))
    place = lax.broadcasted_iota(jnp.int32, (48, 128), 0)
    keys = jnp.zeros((48, 128), jnp.int32)
    for t in range(48):
        ends = jnp.where(wide < 64, ids[first_col + t], ids[first_col + 48 + t])
        keys = jnp.where(place == t, ends, keys)
    total = []
    for part in range(3):
        queries = sum(jnp.where(wide % 16 == t, ids[first_row + part * 16 + t], 0) for t in range(16))
        total.append(jnp.where(keys == queries, gains, 0.0))
    total = jnp.concatenate(total, axis=0)
    for t in range(16):
        rows = []
        for part in range(3):
            start = (part * 16 + t) * 96
            rows.append(jnp.concatenate([normed[start : start + 48, :], normed[start + 48 : start + 96, :]], axis=1))
        here = lane % 16 == t
        weights = jnp.concatenate(
            [jnp.where(here & (lane < 64), w_lanes, 0.0), jnp.where(here & (lane >= 64), w_lanes, 0.0)], axis=0
        )
        total = total + jnp.dot(
            jnp.concatenate(rows, axis=0), weights, precision=lax.Precision.HIGHEST, preferred_element_type=F32
        )
    for part in range(3):
        before = lax.rem(lax.axis_index(ROW) * 3 + part, 8)
        out_ref[part * 48 : part * 48 + 48] = pltpu.roll(total[part * 48 : part * 48 + 48], before * 16, 1)


def project(x, mask, w_query, w_key, w_value, w_gate, gain, query, key, value, gate):
    normed_high, normed_low = split(layer_norm(x, gain))
    normed = jnp.concatenate([normed_high, normed_low], axis=1)

    def turned(weights):
        both = lax.dot_general(weights[...], normed, NT, preferred_element_type=F32)
        return both[:128] + both[128:]

    key_proj = halves(jnp.dot(normed, w_key[...], preferred_element_type=F32))
    query_high, query_low = split(turned(w_query))
    value_high, value_low = split(turned(w_value))
    gate[0] = jax.nn.sigmoid(turned(w_gate))
    block = lax.broadcasted_iota(jnp.int32, (1, 128), 1) // 32
    masked = jnp.broadcast_to(mask - 1.0, (N, 128))
    key_high = key_proj.astype(BF16).astype(F32)
    key_low = pltpu.roll(key_proj - key_high, 64, 1)
    key_again = pltpu.roll(key_high, 32, 1)
    place = lax.broadcasted_iota(jnp.int32, (32, N), 0)
    weight = jnp.where(
        place == 0, 1442840576.0, jnp.where(place == 1, -145408.0, jnp.where(place == 2, -128.0, 0.0))
    ).astype(BF16)
    ones = jnp.ones((16, N), BF16)
    for head in range(HEADS):
        at = [(head + t) % 4 for t in range(4)]
        part = slice(head * 32, (head + 1) * 32)
        key[0, head] = jnp.where(
            block == at[0],
            key_high,
            jnp.where(block == at[1], key_again, jnp.where(block == at[2], key_low, masked)),
        ).astype(BF16)
        rows = [None] * 4
        rows[at[0]] = query_high[part]
        rows[at[1]] = query_low[part]
        rows[at[2]] = query_high[part]
        rows[at[3]] = weight
        query[0, head] = jnp.concatenate(rows, axis=0)
        value[0, head] = jnp.concatenate([value_high[part], value_low[part], ones], axis=0)


def attend(t, query, key, value, gate, bias, w_out, mixed):
    width = 256
    for head in range(HEADS):
        for start in range(0, N, width):
            span = slice(start, start + width)
            scores = jnp.dot(key[t, head], query[t, head, :, span], preferred_element_type=F32)
            scores = scores + bias[head, :, span]
            weights = jnp.exp2(scores - jnp.max(scores, axis=0, keepdims=True))
            high, low = split(weights)
            total = jnp.dot(value[t, head], high, preferred_element_type=F32)
            total = total + jnp.dot(value[t, head], low, preferred_element_type=F32)
            mixed[t, head * 32 : (head + 1) * 32, span] = (total[:32] + total[32:64]) / total[64:65]
    gated_high, gated_low = split(gate[t] * mixed[t])
    gated = jnp.concatenate([gated_high, gated_low], axis=0)
    return halves(lax.dot_general(gated, w_out[...], TN, preferred_element_type=F32))


def start_project_kernel(x_ref, mask_ref, w_query, w_key, w_value, w_gate, gain, query, key, value, gate):
    x = x_ref[...].reshape(N, 128)
    held = mask_ref[:, pl.ds(pl.program_id(0), 1), :].reshape(8, 128).T
    mask = jnp.concatenate([held[:96, part : part + 1] for part in range(8)], axis=0)
    project(x, mask, w_query, w_key, w_value, w_gate, gain[...], query, key, value, gate)


def end_project_kernel(x_ref, w_query, w_key, w_value, w_gate, gain, query, key, value, gate, line_ref, line, mask):
    step = pl.program_id(0)
    lane = lax.broadcasted_iota(jnp.int32, (1, 128), 1)
    for group in range(16):
        held = x_ref[pl.ds(group * 8 * SLOT + LINES * LINES, 8, stride=SLOT), :]
        for t in range(LINES):
            place = pl.ds(group * 8 * LINES + t, 8, stride=LINES)
            line[place, :] = x_ref[pl.ds(group * 8 * SLOT + t * LINES + step, 8, stride=SLOT), :]
            own = jnp.sum(jnp.where(lane == t * LINES + step, held, 0.0), axis=1, keepdims=True)
            mask[place, :] = jnp.broadcast_to(own, (8, 128))
    x = line[...]
    line_ref[0] = x
    project(x, mask[...], w_query, w_key, w_value, w_gate, gain[...], query, key, value, gate)


def start_kernel(
    x_ref, mask_ref, query, key, value, gate, gathered, w_out, end_gain, w_bias, chain_gain, same,
    pair_ref, bias_ref, bias, mixed, line, held, sems,
):
    step = pl.program_id(0)

    @pl.when(step == 0)
    def _():
        copies = fetch(gathered, held, sems)
        pair_ref[...] = jnp.zeros_like(pair_ref)
        for group in range(16):
            pair_ref[pl.ds(group * 8 * SLOT + LINES * LINES, 8, stride=SLOT), :] = mask_ref[group * 8 : group * 8 + 8]
        order_tiles(copies, held, bias)

    place = lax.broadcasted_iota(jnp.int32, (8, 1), 0)
    chain = sum(jnp.where(place == t, chain_gain[1, t], 0.0) for t in range(HEADS))
    for t in range(PAIR):
        first = x_ref[...].reshape(N, 128) + attend(t, query, key, value, gate, bias, w_out, mixed)
        here = step * PAIR + t
        for row in range(16):
            for col in range(8):
                from_row = col * 96 + row * LINES
                pair_ref[pl.ds((row * 8 + col) * SLOT + here * LINES, LINES), :] = first[from_row : from_row + LINES, :]
        normed = layer_norm(first, end_gain[...])
        plane = lax.dot_general(
            w_bias[...], normed, NT, precision=lax.Precision.HIGHEST, preferred_element_type=F32
        )
        plane = (plane + chain * same[t]) * LOG2E
        for head in range(HEADS):
            bias_ref[pl.ds(head * LINES + here, 1), :] = plane[head : head + 1]


def end_kernel(x_ref, query, key, value, gate, gathered, w_out, out_ref, bias, mixed, held, sems):
    @pl.when(pl.program_id(0) == 0)
    def _():
        order_lines(fetch(gathered, held, sems), held, bias)

    for t in range(PAIR):
        update = attend(t, query, key, value, gate, bias, w_out, mixed)
        out_ref[:, t] = (x_ref[t] + update).reshape(16, 48, 128)


def whole(shape):
    return pl.BlockSpec(shape, lambda i: (0,) * len(shape), pipeline_mode=pl.Buffered(1))


def lines(*shape, count=1):
    return pl.BlockSpec((count, *shape), lambda i: (i,) + (0,) * len(shape))


def projected(count):
    shapes = [(HEADS, 128, N), (HEADS, N, 128), (HEADS, 80, N), (128, N)]
    return [lines(*shape, count=count) for shape in shapes]


MATRIX = whole((256, 256))
PROJECTED_SHAPES = [
    jax.ShapeDtypeStruct((LINES, HEADS, 128, N), BF16),
    jax.ShapeDtypeStruct((LINES, HEADS, N, 128), BF16),
    jax.ShapeDtypeStruct((LINES, HEADS, 80, N), BF16),
    jax.ShapeDtypeStruct((LINES, 128, N), F32),
]
PARAMS = pltpu.CompilerParams(vmem_limit_bytes=56 * 1024 * 1024)


def doubled(weights):
    high = lax.reduce_precision(weights, 8, 7)
    both = jnp.concatenate([high, weights - high], axis=1)
    return jnp.concatenate([both, both], axis=0).astype(BF16)


def prepared(w_proj, w_out):
    w_query = doubled(w_proj[:, :128] * (32 ** -0.5 * LOG2E)).T
    w_key = doubled(w_proj[:, 128:256])
    w_value = doubled(w_proj[:, 256:384]).T
    w_gate = doubled(w_proj[:, 384:]).T
    return w_query, w_key, w_value, w_gate, doubled(w_out)


def local(pair_state, pair_mask, chain_ids, ln_gain, w_proj, w_bias, w_out, chain_gain):
    row, col = lax.axis_index(ROW), lax.axis_index(COL)
    tile_bias, parts = pl.pallas_call(
        tile_kernel,
        out_shape=(jax.ShapeDtypeStruct((144, 128), F32), jax.ShapeDtypeStruct((8, PART, 128), F32)),
        in_specs=[
            pl.BlockSpec(memory_space=pltpu.SMEM),
            pl.BlockSpec(memory_space=pltpu.SMEM),
            pl.BlockSpec(memory_space=pltpu.VMEM),
            pl.BlockSpec(memory_space=pltpu.VMEM),
            pl.BlockSpec(memory_space=pltpu.VMEM),
            pl.BlockSpec(memory_space=pltpu.VMEM),
        ],
        scratch_shapes=[pltpu.VMEM((48 * 96, 128), F32)],
        compiler_params=PARAMS,
        name="tile_bias",
    )(chain_ids, chain_gain, pair_state, pair_mask, ln_gain, jnp.swapaxes(w_bias, 1, 2))
    start_bias = gather_start(tile_bias)

    rows = lax.all_to_all(parts, COL, split_axis=0, concat_axis=0, tiled=True)
    sent_mask = rows[:, LINES * 96 : LINES * 97, :96].reshape(8, LINES, 16, LINES)
    sent_mask = jnp.transpose(sent_mask, (2, 0, 1, 3)).reshape(128, LINES * LINES)
    sent_mask = jnp.pad(sent_mask, ((0, 0), (0, 128 - LINES * LINES)))

    *start_weights, start_out = prepared(w_proj[0], w_out[0])
    *end_weights, end_out = prepared(w_proj[1], w_out[1])
    row_block = pl.BlockSpec((8, 96, 128), lambda i: (0, i, 0))
    start_parts = pl.pallas_call(
        start_project_kernel,
        grid=(LINES,),
        out_shape=PROJECTED_SHAPES,
        in_specs=[row_block, pl.BlockSpec((8, 8, 128), lambda i: (0, 72, 0)), MATRIX, MATRIX, MATRIX, MATRIX, whole((1, 128))],
        out_specs=projected(1),
        compiler_params=PARAMS,
        name="start_projections",
    )(rows, rows, *start_weights, ln_gain[0:1])

    ids_line = lax.dynamic_slice(chain_ids, (row * 48 + col * LINES,), (LINES,))
    same_line = (ids_line[:, None] == chain_ids[None, :]).astype(F32).reshape(LINES, 1, N)
    end_w = jnp.concatenate([w_bias[1].T, jnp.zeros((4, 128), F32)], axis=0)
    first_pair, end_shard = pl.pallas_call(
        start_kernel,
        grid=(LINES // PAIR,),
        out_shape=(
            jax.ShapeDtypeStruct((128 * SLOT, 128), F32),
            jax.ShapeDtypeStruct((HEADS * LINES, N), F32),
        ),
        in_specs=[
            row_block, whole((128, 128)),
            *projected(PAIR), pl.BlockSpec(memory_space=pl.ANY), MATRIX,
            whole((1, 128)), whole((8, 128)), pl.BlockSpec(memory_space=pltpu.SMEM), lines(1, N, count=PAIR),
        ],
        out_specs=(whole((128 * SLOT, 128)), whole((HEADS * LINES, N))),
        scratch_shapes=[
            pltpu.VMEM((HEADS, N, N), F32),
            pltpu.VMEM((PAIR, 128, N), F32),
            pltpu.VMEM((PAIR, N, 128), F32),
            pltpu.VMEM((128 * 144, 128), F32),
            pltpu.SemaphoreType.DMA((8,)),
        ],
        compiler_params=PARAMS,
        name="start_attention",
    )(rows, sent_mask, *start_parts, start_bias, start_out, ln_gain[1:2], end_w, chain_gain, same_line)

    end_bias = gather_end(end_shard)
    columns = lax.all_to_all(
        first_pair.reshape(128, SLOT, 128), EVERY, split_axis=0, concat_axis=0, tiled=True
    ).reshape(128 * SLOT, 128)
    *end_parts, end_lines = pl.pallas_call(
        end_project_kernel,
        grid=(LINES,),
        out_shape=PROJECTED_SHAPES + [jax.ShapeDtypeStruct((LINES, N, 128), F32)],
        in_specs=[whole((128 * SLOT, 128)), MATRIX, MATRIX, MATRIX, MATRIX, whole((1, 128))],
        out_specs=projected(1) + [lines(N, 128)],
        scratch_shapes=[pltpu.VMEM((N, 128), F32), pltpu.VMEM((N, 128), F32)],
        compiler_params=PARAMS,
        name="end_projections",
    )(columns, *end_weights, ln_gain[1:2])
    second = pl.pallas_call(
        end_kernel,
        grid=(LINES // PAIR,),
        out_shape=jax.ShapeDtypeStruct((16, LINES, 48, 128), F32),
        in_specs=[lines(N, 128, count=PAIR), *projected(PAIR), pl.BlockSpec(memory_space=pl.ANY), MATRIX],
        out_specs=pl.BlockSpec((16, PAIR, 48, 128), lambda i: (0, i, 0, 0)),
        scratch_shapes=[
            pltpu.VMEM((HEADS, N, N), F32),
            pltpu.VMEM((PAIR, 128, N), F32),
            pltpu.VMEM((128 * 24, N), F32),
            pltpu.SemaphoreType.DMA((8,)),
        ],
        compiler_params=PARAMS,
        name="end_attention",
    )(end_lines, *end_parts, end_bias, end_out)
    returned = lax.all_to_all(second, ROW, split_axis=0, concat_axis=0, tiled=True)
    return jnp.transpose(returned, (2, 0, 1, 3)).reshape(48, 96, 128)


def solution(mesh):
    parts = Mesh(mesh.devices.reshape(4, 2, 2, 4, 2), ("z", "x_hi", "core", "y", "x_lo"))
    return jax.shard_map(
        local,
        mesh=parts,
        in_specs=(P(ROW, COL, None), P(ROW, COL), P(), P(), P(), P(), P(), P()),
        out_specs=P(ROW, COL, None),
        check_vma=False,
    )
```

```python
import functools
import jax
import jax.numpy as jnp
from jax import lax
from jax.experimental import pallas as pl
from jax.experimental.pallas import tpu as pltpu
from jax.sharding import Mesh, PartitionSpec as P

N = 768
HEADS = 4
LINES = 6
SLOT = 40
PART = 584
PAIR = 1
LOG2E = 1.4426950408889634
F32 = jnp.float32
BF16 = jnp.bfloat16
ROW = ("z", "x_hi", "core")
COL = ("y", "x_lo")
EVERY = ROW + COL
NT = (((1,), (1,)), ((), ()))
TN = (((0,), (0,)), ((), ()))


def split(values):
    high = values.astype(BF16)
    return high, (values - high.astype(F32)).astype(BF16)


def layer_norm(values, scales):
    average = jnp.mean(values, axis=-1, keepdims=True)
    centred = values - average
    variance = jnp.mean(centred * centred, axis=-1, keepdims=True)
    return centred * lax.rsqrt(variance + 1e-05) * scales


def halves(values):
    return values[:, :128] + values[:, 128:]


def start_place(row, col):
    ahead = lax.rem(col // 2 + 4 - lax.axis_index("y"), 4)
    along_y = jnp.where(ahead == 0, 0, jnp.where(ahead == 1, 2, jnp.where(ahead == 2, 3, 1)))
    return ((row // 2 * 2 + col % 2) * 2 + row % 2) * 4 + along_y


def gather_start(shard):
    received = [lax.ppermute(shard, "y", [(t, (t + hop) % 4) for t in range(4)]) for hop in (1, 3, 2)]
    blocks = jnp.concatenate([shard, *received], axis=0)
    return lax.all_gather(blocks, ("z", "x_hi", "x_lo", "core"), axis=0, tiled=True)


def end_place(row, col):
    return (row // 2) * 16 + (col % 2) * 8 + (col // 2) * 2 + row % 2


def gather_end(shard):
    return lax.all_gather(shard, ("z", "x_hi", "x_lo", "y", "core"), axis=0, tiled=True)


def fetch(gathered, held, sems):
    size = held.shape[0] // 8
    copies = []
    for t in range(8):
        inside = pl.ds(t * size, size)
        copies.append(pltpu.make_async_copy(gathered.at[inside], held.at[inside], sems.at[t]))
        copies[-1].start()
    return copies


def order_tiles(copies, held, bias):
    slot = lax.broadcasted_iota(jnp.int32, (1, 128), 1) // 16
    arrived = 0
    for tile in range(6):
        while arrived <= (tile * 8 + 7) // 3 // 2:
            copies[arrived].wait()
            arrived += 1

        def step(col, _):
            pieces = []
            for t in range(8):
                row, part = divmod(tile * 8 + t, 3)
                start = pl.multiple_of(start_place(row, col) * 144 + part * 48, 8)
                pieces.append(held[pl.ds(start, 48), :])
            for hop in (1, 2, 4):
                upper = (slot // hop) % 2 == 1
                pieces = [jnp.where(upper, pieces[(t + hop) % 8], pieces[t]) for t in range(8)]
            for t in range(8):
                start = pl.multiple_of(col * 96 + (t // 4) * 48, 8)
                turned = pieces[(8 - t) % 8]
                if t:
                    turned = pltpu.roll(turned, 128 - 16 * t, 1)
                bias[t % 4, pl.ds(start, 48), tile * 128 : (tile + 1) * 128] = turned
            return 0

        lax.fori_loop(0, 8, step, 0)


def order_lines(copies, held, bias):
    for outer in range(8):
        copies[outer].wait()
        for part in range(4):
            owners = [end_place(outer * 2 + part // 2, (part % 2) * 4 + t) for t in range(4)]
            blocks = [held[owner * 24 : owner * 24 + 24, :] for owner in owners]
            start = outer * 96 + part * 24
            for head in range(HEADS):
                rows = [block[head * LINES : (head + 1) * LINES] for block in blocks]
                bias[head, start : start + 24, :] = jnp.concatenate(rows, axis=0)


def tile_kernel(ids, chain_gain, pair_ref, mask_ref, gain, w_bias, out_ref, parts, normed, masks, sems):
    mask = jnp.concatenate([mask_ref[...].astype(F32), jnp.zeros((48, 32), F32)], axis=1)
    size = LINES * 96
    for part in range(8):
        inside = slice(part * LINES, (part + 1) * LINES)
        masks[part] = jnp.concatenate([mask[inside], jnp.zeros((2, 128), F32)], axis=0)
    copies = []
    for part in range(8):
        pairs = pair_ref.at[pl.ds(part * size, size)]
        copies.append(pltpu.make_async_copy(pairs, parts.at[part, pl.ds(0, size)], sems.at[part]))
        copies.append(pltpu.make_async_copy(masks.at[part], parts.at[part, pl.ds(size, 8)], sems.at[8 + part]))
    for copy in copies:
        copy.start()
    normed[...] = layer_norm(pair_ref[...], gain[:1])
    lane = lax.broadcasted_iota(jnp.int32, (128, 128), 1)
    head = (lane // 16) % 4
    columns = jnp.concatenate([w_bias[0], w_bias[0]], axis=0).T
    w_lanes = sum(jnp.where(head == t, columns[:, t : t + 1] * LOG2E, 0.0) for t in range(HEADS))
    first_row, first_col = lax.axis_index(ROW) * 48, lax.axis_index(COL) * 96
    wide = lane[:1]
    gains = sum(jnp.where(head[:1] == t, chain_gain[0, t] * LOG2E, 0.0) for t in range(HEADS))
    place = lax.broadcasted_iota(jnp.int32, (48, 128), 0)
    keys = jnp.zeros((48, 128), jnp.int32)
    for t in range(48):
        ends = jnp.where(wide < 64, ids[first_col + t], ids[first_col + 48 + t])
        keys = jnp.where(place == t, ends, keys)
    total = []
    for part in range(3):
        queries = sum(jnp.where(wide % 16 == t, ids[first_row + part * 16 + t], 0) for t in range(16))
        total.append(jnp.where(keys == queries, gains, 0.0))
    total = jnp.concatenate(total, axis=0)
    for t in range(16):
        rows = []
        for part in range(3):
            start = (part * 16 + t) * 96
            rows.append(jnp.concatenate([normed[start : start + 48, :], normed[start + 48 : start + 96, :]], axis=1))
        here = lane % 16 == t
        weights = jnp.concatenate(
            [jnp.where(here & (lane < 64), w_lanes, 0.0), jnp.where(here & (lane >= 64), w_lanes, 0.0)], axis=0
        )
        total = total + jnp.dot(
            jnp.concatenate(rows, axis=0), weights, precision=lax.Precision.HIGHEST, preferred_element_type=F32
        )
    for part in range(3):
        before = lax.rem(lax.axis_index(ROW) * 3 + part, 8)
        out_ref[part * 48 : part * 48 + 48] = pltpu.roll(total[part * 48 : part * 48 + 48], before * 16, 1)
    for copy in copies:
        copy.wait()


def project(x, mask, w_query, w_key, w_value, w_gate, gain, query, key, value, gate):
    normed_high, normed_low = split(layer_norm(x, gain))
    normed = jnp.concatenate([normed_high, normed_low], axis=1)

    def turned(weights):
        both = lax.dot_general(weights[...], normed, NT, preferred_element_type=F32)
        return both[:128] + both[128:]

    key_proj = halves(jnp.dot(normed, w_key[...], preferred_element_type=F32))
    query_high, query_low = split(turned(w_query))
    value_high, value_low = split(turned(w_value))
    gate[0] = jax.nn.sigmoid(turned(w_gate))
    block = lax.broadcasted_iota(jnp.int32, (1, 128), 1) // 32
    masked = jnp.broadcast_to(mask - 1.0, (N, 128))
    key_high = key_proj.astype(BF16).astype(F32)
    key_low = pltpu.roll(key_proj - key_high, 64, 1)
    key_again = pltpu.roll(key_high, 32, 1)
    place = lax.broadcasted_iota(jnp.int32, (32, N), 0)
    weight = jnp.where(
        place == 0, 1442840576.0, jnp.where(place == 1, -145408.0, jnp.where(place == 2, -128.0, 0.0))
    ).astype(BF16)
    ones = jnp.ones((16, N), BF16)
    for head in range(HEADS):
        at = [(head + t) % 4 for t in range(4)]
        part = slice(head * 32, (head + 1) * 32)
        key[0, head] = jnp.where(
            block == at[0],
            key_high,
            jnp.where(block == at[1], key_again, jnp.where(block == at[2], key_low, masked)),
        ).astype(BF16)
        rows = [None] * 4
        rows[at[0]] = query_high[part]
        rows[at[1]] = query_low[part]
        rows[at[2]] = query_high[part]
        rows[at[3]] = weight
        query[0, head] = jnp.concatenate(rows, axis=0)
        value[0, head] = jnp.concatenate([value_high[part], value_low[part], ones], axis=0)


def attend(t, query, key, value, gate, bias, w_out, mixed):
    width = 256
    for head in range(HEADS):
        for start in range(0, N, width):
            span = slice(start, start + width)
            scores = jnp.dot(key[t, head], query[t, head, :, span], preferred_element_type=F32)
            scores = scores + bias[head, :, span]
            weights = jnp.exp2(scores - jnp.max(scores, axis=0, keepdims=True))
            high, low = split(weights)
            total = jnp.dot(value[t, head], high, preferred_element_type=F32)
            total = total + jnp.dot(value[t, head], low, preferred_element_type=F32)
            mixed[t, head * 32 : (head + 1) * 32, span] = (total[:32] + total[32:64]) / total[64:65]
    gated_high, gated_low = split(gate[t] * mixed[t])
    gated = jnp.concatenate([gated_high, gated_low], axis=0)
    return halves(lax.dot_general(gated, w_out[...], TN, preferred_element_type=F32))


def start_project_kernel(x_ref, mask_ref, w_query, w_key, w_value, w_gate, gain, query, key, value, gate):
    x = x_ref[...].reshape(N, 128)
    held = mask_ref[:, pl.ds(pl.program_id(0), 1), :].reshape(8, 128).T
    mask = jnp.concatenate([held[:96, part : part + 1] for part in range(8)], axis=0)
    project(x, mask, w_query, w_key, w_value, w_gate, gain[...], query, key, value, gate)


def end_project_kernel(x_ref, w_query, w_key, w_value, w_gate, gain, query, key, value, gate, line_ref, line, mask):
    step = pl.program_id(0)
    lane = lax.broadcasted_iota(jnp.int32, (1, 128), 1)
    for group in range(16):
        held = x_ref[pl.ds(group * 8 * SLOT + LINES * LINES, 8, stride=SLOT), :]
        for t in range(LINES):
            place = pl.ds(group * 8 * LINES + t, 8, stride=LINES)
            line[place, :] = x_ref[pl.ds(group * 8 * SLOT + t * LINES + step, 8, stride=SLOT), :]
            own = jnp.sum(jnp.where(lane == t * LINES + step, held, 0.0), axis=1, keepdims=True)
            mask[place, :] = jnp.broadcast_to(own, (8, 128))
    x = line[...]
    line_ref[0] = x
    project(x, mask[...], w_query, w_key, w_value, w_gate, gain[...], query, key, value, gate)


def start_kernel(
    x_ref, mask_ref, query, key, value, gate, gathered, w_out, end_gain, w_bias, chain_gain, same,
    pair_ref, bias_ref, bias, mixed, line, held, sems,
):
    step = pl.program_id(0)

    @pl.when(step == 0)
    def _():
        copies = fetch(gathered, held, sems)
        for group in range(16):
            pair_ref[pl.ds(group * 8 * SLOT + LINES * LINES, 8, stride=SLOT), :] = mask_ref[group * 8 : group * 8 + 8]
            for unused in range(LINES * LINES + 1, SLOT):
                pair_ref[pl.ds(group * 8 * SLOT + unused, 8, stride=SLOT), :] = jnp.zeros((8, 128), F32)
        order_tiles(copies, held, bias)

    place = lax.broadcasted_iota(jnp.int32, (8, 1), 0)
    chain = sum(jnp.where(place == t, chain_gain[1, t], 0.0) for t in range(HEADS))
    for t in range(PAIR):
        first = x_ref[...].reshape(N, 128) + attend(t, query, key, value, gate, bias, w_out, mixed)
        here = step * PAIR + t
        for row in range(16):
            for col in range(8):
                from_row = col * 96 + row * LINES
                pair_ref[pl.ds((row * 8 + col) * SLOT + here * LINES, LINES), :] = first[from_row : from_row + LINES, :]
        normed = layer_norm(first, end_gain[...])
        plane = lax.dot_general(
            w_bias[...], normed, NT, precision=lax.Precision.HIGHEST, preferred_element_type=F32
        )
        plane = (plane + chain * same[t]) * LOG2E
        for head in range(HEADS):
            bias_ref[pl.ds(head * LINES + here, 1), :] = plane[head : head + 1]


def end_kernel(x_ref, query, key, value, gate, gathered, w_out, out_ref, bias, mixed, held, sems):
    @pl.when(pl.program_id(0) == 0)
    def _():
        order_lines(fetch(gathered, held, sems), held, bias)

    for t in range(PAIR):
        update = attend(t, query, key, value, gate, bias, w_out, mixed)
        out_ref[:, t] = (x_ref[t] + update).reshape(16, 48, 128)


def whole(shape):
    return pl.BlockSpec(shape, lambda i: (0,) * len(shape), pipeline_mode=pl.Buffered(1))


def lines(*shape, count=1):
    return pl.BlockSpec((count, *shape), lambda i: (i,) + (0,) * len(shape))


def projected(count):
    shapes = [(HEADS, 128, N), (HEADS, N, 128), (HEADS, 80, N), (128, N)]
    return [lines(*shape, count=count) for shape in shapes]


MATRIX = whole((256, 256))
PROJECTED_SHAPES = [
    jax.ShapeDtypeStruct((LINES, HEADS, 128, N), BF16),
    jax.ShapeDtypeStruct((LINES, HEADS, N, 128), BF16),
    jax.ShapeDtypeStruct((LINES, HEADS, 80, N), BF16),
    jax.ShapeDtypeStruct((LINES, 128, N), F32),
]
PARAMS = pltpu.CompilerParams(vmem_limit_bytes=56 * 1024 * 1024)


def doubled(weights):
    high = lax.reduce_precision(weights, 8, 7)
    both = jnp.concatenate([high, weights - high], axis=1)
    return jnp.concatenate([both, both], axis=0).astype(BF16)


def prepared(w_proj, w_out):
    w_query = doubled(w_proj[:, :128] * (32 ** -0.5 * LOG2E)).T
    w_key = doubled(w_proj[:, 128:256])
    w_value = doubled(w_proj[:, 256:384]).T
    w_gate = doubled(w_proj[:, 384:]).T
    return w_query, w_key, w_value, w_gate, doubled(w_out)


def local(pair_state, pair_mask, chain_ids, ln_gain, w_proj, w_bias, w_out, chain_gain):
    row, col = lax.axis_index(ROW), lax.axis_index(COL)
    tile_bias, parts = pl.pallas_call(
        tile_kernel,
        out_shape=(jax.ShapeDtypeStruct((144, 128), F32), jax.ShapeDtypeStruct((8, PART, 128), F32)),
        in_specs=[
            pl.BlockSpec(memory_space=pltpu.SMEM),
            pl.BlockSpec(memory_space=pltpu.SMEM),
            pl.BlockSpec(memory_space=pltpu.VMEM),
            pl.BlockSpec(memory_space=pltpu.VMEM),
            pl.BlockSpec(memory_space=pltpu.VMEM),
            pl.BlockSpec(memory_space=pltpu.VMEM),
        ],
        out_specs=(pl.BlockSpec(memory_space=pltpu.VMEM), pl.BlockSpec(memory_space=pl.ANY)),
        scratch_shapes=[
            pltpu.VMEM((48 * 96, 128), F32),
            pltpu.VMEM((8, 8, 128), F32),
            pltpu.SemaphoreType.DMA((16,)),
        ],
        compiler_params=PARAMS,
        name="tile_bias",
    )(chain_ids, chain_gain, pair_state.reshape(48 * 96, 128), pair_mask, ln_gain, jnp.swapaxes(w_bias, 1, 2))
    start_bias = gather_start(tile_bias)

    rows = lax.all_to_all(parts, COL, split_axis=0, concat_axis=0, tiled=True)
    sent_mask = rows[:, LINES * 96 : LINES * 97, :96].reshape(8, LINES, 16, LINES)
    sent_mask = jnp.transpose(sent_mask, (2, 0, 1, 3)).reshape(128, LINES * LINES)
    sent_mask = jnp.pad(sent_mask, ((0, 0), (0, 128 - LINES * LINES)))

    *start_weights, start_out = prepared(w_proj[0], w_out[0])
    *end_weights, end_out = prepared(w_proj[1], w_out[1])
    row_block = pl.BlockSpec((8, 96, 128), lambda i: (0, i, 0))
    start_parts = pl.pallas_call(
        start_project_kernel,
        grid=(LINES,),
        out_shape=PROJECTED_SHAPES,
        in_specs=[row_block, pl.BlockSpec((8, 8, 128), lambda i: (0, 72, 0)), MATRIX, MATRIX, MATRIX, MATRIX, whole((1, 128))],
        out_specs=projected(1),
        compiler_params=PARAMS,
        name="start_projections",
    )(rows, rows, *start_weights, ln_gain[0:1])

    ids_line = lax.dynamic_slice(chain_ids, (row * 48 + col * LINES,), (LINES,))
    same_line = (ids_line[:, None] == chain_ids[None, :]).astype(F32).reshape(LINES, 1, N)
    end_w = jnp.concatenate([w_bias[1].T, jnp.zeros((4, 128), F32)], axis=0)
    first_pair, end_shard = pl.pallas_call(
        start_kernel,
        grid=(LINES // PAIR,),
        out_shape=(
            jax.ShapeDtypeStruct((128 * SLOT, 128), F32),
            jax.ShapeDtypeStruct((HEADS * LINES, N), F32),
        ),
        in_specs=[
            row_block, whole((128, 128)),
            *projected(PAIR), pl.BlockSpec(memory_space=pl.ANY), MATRIX,
            whole((1, 128)), whole((8, 128)), pl.BlockSpec(memory_space=pltpu.SMEM), lines(1, N, count=PAIR),
        ],
        out_specs=(whole((128 * SLOT, 128)), whole((HEADS * LINES, N))),
        scratch_shapes=[
            pltpu.VMEM((HEADS, N, N), F32),
            pltpu.VMEM((PAIR, 128, N), F32),
            pltpu.VMEM((PAIR, N, 128), F32),
            pltpu.VMEM((128 * 144, 128), F32),
            pltpu.SemaphoreType.DMA((8,)),
        ],
        compiler_params=PARAMS,
        name="start_attention",
    )(rows, sent_mask, *start_parts, start_bias, start_out, ln_gain[1:2], end_w, chain_gain, same_line)

    end_bias = gather_end(end_shard)
    columns = lax.all_to_all(
        first_pair.reshape(128, SLOT, 128), EVERY, split_axis=0, concat_axis=0, tiled=True
    ).reshape(128 * SLOT, 128)
    *end_parts, end_lines = pl.pallas_call(
        end_project_kernel,
        grid=(LINES,),
        out_shape=PROJECTED_SHAPES + [jax.ShapeDtypeStruct((LINES, N, 128), F32)],
        in_specs=[whole((128 * SLOT, 128)), MATRIX, MATRIX, MATRIX, MATRIX, whole((1, 128))],
        out_specs=projected(1) + [lines(N, 128)],
        scratch_shapes=[pltpu.VMEM((N, 128), F32), pltpu.VMEM((N, 128), F32)],
        compiler_params=PARAMS,
        name="end_projections",
    )(columns, *end_weights, ln_gain[1:2])
    second = pl.pallas_call(
        end_kernel,
        grid=(LINES // PAIR,),
        out_shape=jax.ShapeDtypeStruct((16, LINES, 48, 128), F32),
        in_specs=[lines(N, 128, count=PAIR), *projected(PAIR), pl.BlockSpec(memory_space=pl.ANY), MATRIX],
        out_specs=pl.BlockSpec((16, PAIR, 48, 128), lambda i: (0, i, 0, 0)),
        scratch_shapes=[
            pltpu.VMEM((HEADS, N, N), F32),
            pltpu.VMEM((PAIR, 128, N), F32),
            pltpu.VMEM((128 * 24, N), F32),
            pltpu.SemaphoreType.DMA((8,)),
        ],
        compiler_params=PARAMS,
        name="end_attention",
    )(end_lines, *end_parts, end_bias, end_out)
    returned = lax.all_to_all(second, ROW, split_axis=0, concat_axis=0, tiled=True)
    return jnp.transpose(returned, (2, 0, 1, 3)).reshape(48, 96, 128)


def solution(mesh):
    parts = Mesh(mesh.devices.reshape(4, 2, 2, 4, 2), ("z", "x_hi", "core", "y", "x_lo"))
    return jax.shard_map(
        local,
        mesh=parts,
        in_specs=(P(ROW, COL, None), P(ROW, COL), P(), P(), P(), P(), P(), P()),
        out_specs=P(ROW, COL, None),
        check_vma=False,
    )
```
